32 devices in a mesh: pole: 2 (over x), row: 4 (over y, core), col: 4 (over z).
Axes of the slice: x: 2, y: 2, z: 4, core: 2. Of those that a mesh axis runs over, the one named last changes fastest.
Arguments:
- inverse_tile: float32 [2, 2, 4608, 4608], P('pole', None, 'row', 'col'), may hold values from -0.0625 to 0.0625
- lower_factor: float32 [2, 2, 256, 4608], P('pole', None, 'row', 'col'), may hold values from -6 to 6
- upper_factor: float32 [2, 2, 256, 4608], P('pole', None, 'col', 'row'), may hold values from -1.5 to 1.5
- pivot_inverse: float32 [2, 2, 256, 256], P('pole', None, 'row', 'col'), may hold values from -48 to 48
- pole_weights: float32 [2, 2], P('pole'), may hold values from -3 to 3
- block_owners: int32 [576, 6], replicated, may hold values from 0 to 31, all different within a row; in each aligned block of 18 rows (0 to 17, 18 to 35, ...) at most 4 rows name the same one
- basis_ancestor: float32 [4608, 4096], P(None, ('pole', 'row', 'col')), may hold values from -3 to 3
- basis_super: float32 [256, 4096], P(None, ('pole', 'row', 'col')), may hold values from -0.09375 to 0.09375
Outputs:
- upper_density: float32 [256, 4608], P(('pole', 'row'), 'col')
- charge: float32 [4096], P(('pole', 'row', 'col'))
The draws below stay inside these ranges and needn't reach their ends.
Inputs may be any that keep to these rules, and one draw needn't show every extreme that they name: `block_owners`: each row names 6 different owners. Among the rows k * 18 to (k + 1) * 18 - 1, for each k, no owner is named more than 4 times, and in every draw some owner is named exactly 4 times there. Every owner is named by some row.
All inputs are finite; a program needn't handle non-finite values.
Results may differ from the reference program's by a relative error of at most 0.0003.
Values sent between devices are 32-bit elements; how exact they have to be, the bound alone decides.
No kernel may reach another device: no remote copies, remote signals or barrier semaphores. Data moves between devices by JAX's collectives and lax.ppermute only.
A program may use at most 64 MiB of HBM per device.

```python
import math
import jax
import jax.numpy as jnp
import numpy as np
from jax import lax

S = 256
R = 4608
POLES = 2
NB = 18
TOPK = 6
GP = 128
BR = 8
NBLK = 576
CAP = 4
GRID = 4096
DEVICES = 32


def levels(own_key, shape, split, low, largest):
    loudness, own = 1.0, jax.random.fold_in(own_key, 6)
    for axis_at, blocks in split:
        draws = jnp.exp(jax.random.uniform(jax.random.fold_in(own, axis_at), (blocks,), jnp.float32, low / len(split), largest / len(split)))
        loudness = loudness * jnp.repeat(draws, shape[axis_at] // blocks).reshape([-1 if axis == axis_at else 1 for axis in range(len(shape))])
    return loudness


def assign_block(stream_key, own, number, rows, count, top, most, slope):
    ranking = jax.random.permutation(stream_key, count)
    crowded, usual = portions_of(count, rows * top, most, slope, True), portions_of(count, rows * top, most, slope, False)
    places = jnp.arange(count)

    def named(sizes, rotation):
        used = int((sizes > 0).sum())
        fixed = max(1, used // 4)
        moved = fixed + (places - fixed + rotation * (used - fixed)) % max(1, count - fixed)
        return jnp.zeros((count,), jnp.int32).at[ranking[jnp.where(places < fixed, places, moved)]].set(jnp.asarray(sizes, jnp.int32))

    sizes = jnp.where(number % 4 == 0, named(crowded, number // 4), named(usual, number - number // 4 - 1))
    mixed = jax.random.permutation(jax.random.fold_in(own, 3), count)
    source_of, taker = mixed[0:count // 2 * 2:2], mixed[1:count // 2 * 2:2]
    margin = jnp.minimum(sizes[source_of] - 1, most - sizes[taker]) // 2
    margin = jnp.where((source_of == ranking[0]) | (taker == ranking[0]) | (sizes[taker] == 0), 0, jnp.maximum(margin, 0))
    moved = jax.random.randint(jax.random.fold_in(own, 4), (count // 2,), 0, 1 << 20) % (margin + 1)
    sizes = sizes.at[source_of].add(-moved).at[taker].add(moved)
    items = jnp.searchsorted(jnp.cumsum(sizes), jnp.arange(rows * top), side="right").astype(jnp.int32)
    table = items.reshape(top, rows).T
    table = table[jax.random.permutation(jax.random.fold_in(own, 1), rows)]
    rotation = jax.random.randint(jax.random.fold_in(own, 2), (rows, 1), 0, top)
    return jnp.take_along_axis(table, (jnp.arange(top)[None, :] + rotation) % top, axis=1)


def portions_of(count, total, reach, skew, full):
    weights = [(1 << 20) // math.isqrt(standing ** skew) + 1 for standing in range(1, count + 1)]
    largest = reach if full else min(reach, max(-(-total // count), total * weights[0] // sum(weights)))
    least = 1 if total - largest >= count - 1 else 0
    holding, surplus = [largest] + [least] * (count - 1), total - largest - least * (count - 1)
    while surplus > 0:
        free = [i for i in range(1, count) if holding[i] < largest] or [i for i in range(1, count) if holding[i] < reach]
        mass, left = sum([weights[i] for i in free]), surplus
        for i in free:
            more = min(reach - holding[i], max(1, left * weights[i] // mass), surplus)
            holding[i] = holding[i] + more
            surplus = surplus - more
    return np.array(holding)


def noise(rng, shape, width, most, split=(), kind=jnp.bfloat16):
    entries = width * jax.random.normal(rng, shape, jnp.float32)
    if split:
        entries = entries * levels(rng, shape, split, -0.22, 0.18)
    return jnp.clip(entries, -most, most).astype(kind)


def setup_inputs(seed: int = 0) -> dict:
    seeds = jax.random.split(jax.random.key(seed), 9)
    inverse_tile = noise(seeds[0], (POLES, 2, R, R), (2 * R) ** -0.5, 0.0625, ((0, 2), (2, 4), (3, 4)), jnp.float32)
    lower_factor = noise(seeds[1], (POLES, 2, S, R), 1.0, 6.0, ((0, 2), (2, 4), (3, 4)), jnp.float32)
    upper_factor = noise(seeds[2], (POLES, 2, S, R), 0.25, 1.5, ((0, 2), (2, 4), (3, 4)), jnp.float32)
    pivot_inverse = noise(seeds[3], (POLES, 2, S, S), 8.0, 48.0, ((0, 2), (2, 4), (3, 4)), jnp.float32)
    pole_weights = noise(seeds[4], (POLES, 2), 0.5, 3.0, ((0, 2),), jnp.float32)
    block_owners_keys = jax.random.split(jax.random.fold_in(seeds[5], 1), NBLK // NB)
    block_owners_turns = jax.random.permutation(jax.random.fold_in(seeds[5], 3), NBLK // NB)
    block_owners = jax.vmap(lambda own, number: assign_block(jax.random.fold_in(seeds[5], 2), own, number, NB, DEVICES, TOPK, CAP, 2))(block_owners_keys, block_owners_turns).reshape((NBLK, TOPK))
    basis_ancestor = noise(seeds[6], (R, GRID), 0.5, 3.0, ((1, 32),), jnp.float32)
    basis_super = noise(seeds[7], (S, GRID), 4096 ** -0.5, 0.09375, ((1, 32),), jnp.float32)
    return dict(inverse_tile=inverse_tile, lower_factor=lower_factor, upper_factor=upper_factor, pivot_inverse=pivot_inverse, pole_weights=pole_weights, block_owners=block_owners, basis_ancestor=basis_ancestor, basis_super=basis_super)


def product(left, right):
    return jnp.dot(left, right, precision=lax.Precision.HIGHEST, preferred_element_type=jnp.float32)


def product_t(left, right):
    return lax.dot_general(left, right, (((1,), (1,)), ((), ())), precision=lax.Precision.HIGHEST, preferred_element_type=jnp.float32)


def reference(inverse_tile, lower_factor, upper_factor, pivot_inverse, pole_weights, block_owners, basis_ancestor, basis_super):
    def per_pole(carry, items):
        tile, lower_t, upper, pivot, weight = items
        lower_sum, upper_sum, pivot_sum = carry
        al_re = product_t(tile[0], lower_t[0]) - product_t(tile[1], lower_t[1])
        al_im = product_t(tile[0], lower_t[1]) + product_t(tile[1], lower_t[0])
        ua_re = product(upper[0], tile[0]) - product(upper[1], tile[1])
        ua_im = product(upper[0], tile[1]) + product(upper[1], tile[0])
        ual_re = product(upper[0], al_re) - product(upper[1], al_im)
        ual_im = product(upper[0], al_im) + product(upper[1], al_re)
        lower_sum = lower_sum - (weight[0] * al_im + weight[1] * al_re)
        upper_sum = upper_sum - (weight[0] * ua_im + weight[1] * ua_re)
        pivot_sum = pivot_sum + weight[0] * (pivot[1] + ual_im) + weight[1] * (pivot[0] + ual_re)
        return (lower_sum, upper_sum, pivot_sum), None

    start = (jnp.zeros((R, S), jnp.float32), jnp.zeros((S, R), jnp.float32), jnp.zeros((S, S), jnp.float32))
    (lower_density, upper_density, pivot_density), unused = lax.scan(
        per_pole, start, (inverse_tile, lower_factor, upper_factor, pivot_inverse, pole_weights))

    def per_owner(owner):
        routed = jnp.any(block_owners == owner, axis=1).astype(jnp.float32)
        row_mask = jnp.repeat(routed, BR)
        offset = (owner * GP).astype(jnp.int32)
        super_cols = lax.dynamic_slice_in_dim(basis_super, offset, GP, 1)
        ances_cols = lax.dynamic_slice_in_dim(basis_ancestor, offset, GP, 1)
        projected = product(lower_density, super_cols)
        ancestor_part = jnp.sum(row_mask[:, None] * ances_cols * projected, 0)
        pivot_part = jnp.sum(super_cols * product(pivot_density, super_cols), 0)
        return ancestor_part + pivot_part

    charge = lax.map(per_owner, jnp.arange(DEVICES, dtype=jnp.int32)).reshape(GRID)
    return upper_density, charge
```

```python
import jax
import jax.numpy as jnp
from jax import lax
from jax.sharding import PartitionSpec as P

BLOCKS = 18
HIGH = lax.Precision.HIGH


def dot(left, right, contract):
    return lax.dot_general(
        left, right, (contract, ((), ())), precision=HIGH, preferred_element_type=jnp.float32
    )


def permute(x, axis, pairs):
    return lax.ppermute(x, axis, pairs)


def swap(x, axis, mask):
    return lax.ppermute(x, axis, [(i, i ^ mask) for i in range(lax.axis_size(axis))])


def shift(x, axis, by):
    n = lax.axis_size(axis)
    return lax.ppermute(x, axis, [(i, (i + by) % n) for i in range(n)])


def gather_swapped(x, axis):
    n = lax.axis_size(axis)
    held = {0: x}
    bit = n // 2
    while bit:
        held.update({d ^ bit: swap(held[d], axis, bit) for d in list(held)})
        bit //= 2
    return [held[d] for d in range(n)]


def gather_cyclic(x, axis):
    n = lax.axis_size(axis)
    if n != 4:
        return [x] + [shift(x, axis, -p) for p in range(1, n)]
    one, three = shift(x, axis, -1), shift(x, axis, 1)
    leftward = permute(one, axis, [(2, 1), (1, 0)])
    rightward = permute(three, axis, [(1, 2), (2, 3)])
    two = jnp.where(lax.axis_index(axis) < 2, leftward, rightward)
    return [x, one, two, three]


def reduce_scatter_swapped(x, axis, masks):
    total = x[0]
    for term, mask in zip(x[1:], masks, strict=True):
        total = total + swap(term, axis, mask)
    return total


def pick(x, at):
    return lax.dynamic_index_in_dim(x, at, 0, keepdims=False)


def scatter_line(x, axis):
    n = lax.axis_size(axis)
    me = lax.axis_index(axis)
    total = pick(x, me)
    for way in (1, -1):
        arrived = None
        for step in range(1, n):
            at = jnp.mod(me + way * (n - step), n)
            out = pick(x, at)
            if arrived is not None:
                out = out + arrived
            if way > 0:
                pairs = [(i, i + 1) for i in range(step) if i + 1 < n]
            else:
                pairs = [(n - 1 - i, n - 2 - i) for i in range(step) if n - 2 - i >= 0]
            arrived = permute(out, axis, pairs)
        total = total + arrived
    return total


def scatter_swapped(x, axis):
    n = lax.axis_size(axis)
    me = lax.axis_index(axis)
    return reduce_scatter_swapped(
        [pick(x, me ^ d) for d in range(n)], axis, list(range(1, n))
    )


def gather_all(x, axes):
    n = 1
    for axis in axes:
        n *= lax.axis_size(axis)
    spread = jnp.broadcast_to(x[None], (n,) + x.shape)
    return lax.all_to_all(spread, axes, split_axis=0, concat_axis=0, tiled=True)


def body(
    inverse_tile,
    lower_factor,
    upper_factor,
    pivot_inverse,
    pole_weights,
    block_owners,
    basis_ancestor,
    basis_super,
):
    n_pole, n_row, n_col = (lax.axis_size(a) for a in ("pole", "row", "col"))
    pole, row, col = (lax.axis_index(a) for a in ("pole", "row", "col"))
    devices_all = n_pole * n_row * n_col
    weight_re, weight_im = pole_weights[0, 0], pole_weights[0, 1]
    tile_rows, tile_cols = inverse_tile.shape[2:]
    width = basis_super.shape[0]
    piece = lower_factor.shape[2]
    top = block_owners.shape[1]
    capacity = max(2, (BLOCKS * top + devices_all - 1) // devices_all)
    rows_here = tile_rows // (n_pole * n_col)
    block_rows = rows_here // BLOCKS

    lower = gather_swapped(lower_factor[0], "row")
    upper = gather_cyclic(upper_factor[0], "col")

    me = (pole * n_row + row) * n_col + col
    groups = n_row * n_pole * n_col
    hit = jnp.any(block_owners == me, axis=1).reshape(groups, BLOCKS).astype(jnp.int32)
    rank = jnp.cumsum(hit, 1) - hit
    slots = jnp.arange(capacity, dtype=jnp.int32)
    chosen = (rank[:, None, :] == slots[None, :, None]) & (hit[:, None, :] > 0)
    ids = jnp.arange(groups * BLOCKS, dtype=jnp.int32).reshape(groups, 1, BLOCKS)
    slot_ids = jnp.sum(jnp.where(chosen, ids, 0), 2)
    slot_used = jnp.any(chosen, 2)

    def by_device(x):
        x = x.reshape(n_row, n_pole, n_col, capacity)
        return x.transpose(1, 0, 2, 3).reshape(-1)

    slot_ids, slot_used = by_device(slot_ids), by_device(slot_used)
    points = basis_ancestor.shape[1]
    ancestor = jnp.take(
        basis_ancestor.reshape(groups * BLOCKS, block_rows * points), slot_ids, axis=0
    )
    ancestor = jnp.where(slot_used[:, None], ancestor, 0.0).reshape(-1, points)
    position = (row * n_pole + pole) * n_col + col
    owners_here = lax.dynamic_slice_in_dim(block_owners, position * BLOCKS, BLOCKS, 0)
    owned = jnp.any(
        owners_here[:, :, None] == jnp.arange(devices_all, dtype=jnp.int32)[None, None, :], 1
    ).astype(jnp.int32)
    rank_here = jnp.cumsum(owned, 0) - owned
    selector = (
        (owned[:, :, None] > 0) & (rank_here[:, :, None] == slots[None, None, :])
    ).astype(jnp.float32).reshape(BLOCKS, devices_all * capacity)

    tile_re, tile_im = inverse_tile[0, 0], inverse_tile[0, 1]
    lower_re = jnp.concatenate([block[0] for block in lower], 0)
    lower_im = jnp.concatenate([block[1] for block in lower], 0)
    scaled_re = weight_re * lower_re - weight_im * lower_im
    scaled_im = weight_re * lower_im + weight_im * lower_re
    last = ((1,), (1,))
    imag = dot(tile_re, scaled_im, last) + dot(tile_im, scaled_re, last)
    terms = imag.reshape(n_pole, tile_rows // n_pole, width)
    half = scatter_swapped(terms, "pole")
    rows = -scatter_line(half.reshape(n_col, rows_here, width), "col")
    real = dot(tile_re, scaled_re, last) - dot(tile_im, scaled_im, last)

    def ordered(x):
        x = x.reshape(x.shape[0], n_row, piece)
        return jnp.concatenate([pick(x.transpose(1, 0, 2), row ^ d) for d in range(n_row)], 1)

    rows = ordered(rows)
    sent = lax.dot_general(
        selector,
        rows.reshape(BLOCKS, block_rows * width),
        (((0,), (0,)), ((), ())),
        precision=lax.Precision.HIGHEST,
        preferred_element_type=jnp.float32,
    )
    received = lax.all_to_all(
        sent.reshape(devices_all, capacity, block_rows, width),
        ("pole", "row", "col"),
        split_axis=0,
        concat_axis=0,
        tiled=True,
    ).reshape(-1, width)

    upper_re = jnp.concatenate([block[0] for block in upper], 0)
    upper_im = jnp.concatenate([block[1] for block in upper], 0)
    both = jnp.concatenate(
        [
            weight_re * upper_im + weight_im * upper_re,
            weight_re * upper_re - weight_im * upper_im,
        ],
        1,
    )
    product = dot(both, inverse_tile.reshape(2 * tile_rows, tile_cols), ((1,), (0,)))
    out_rows = width // (n_pole * n_row)
    n_far = n_row // 2
    product = product.reshape(n_col, width // n_col, tile_cols)
    product = jnp.concatenate([pick(product, jnp.mod(k - col, n_col)) for k in range(n_col)], 0)
    product = product.reshape(n_pole * n_far, 2, out_rows, tile_cols).transpose(1, 0, 2, 3)
    low, far = row % 2, row // 2
    near = pick(product, low) + swap(pick(product, 1 - low), "row", 1)
    near = near.reshape(n_pole, n_far, out_rows, tile_cols)
    cut = out_rows // 2
    first, second = near[:, :, :cut], near[:, :, cut:]

    def over_far(x):
        return reduce_scatter_swapped(
            [pick(x, far ^ d) for d in range(n_far)], "row", [2 * d for d in range(1, n_far)]
        )

    first = scatter_swapped(over_far(first.transpose(1, 0, 2, 3)), "pole")
    second = over_far(scatter_swapped(second, "pole"))
    upper_density = -jnp.concatenate([first, second], 0)

    pivot = dot(upper_re, imag, ((1,), (0,))) + dot(upper_im, real, ((1,), (0,)))
    pivot = pivot.reshape(n_col, width // n_col, width)
    pivot = jnp.concatenate([pick(pivot, jnp.mod(k - col, n_col)) for k in range(n_col)], 0)
    pivot = ordered(pivot)
    pivot_piece = weight_re * pivot_inverse[0, 1] + weight_im * pivot_inverse[0, 0]
    placed = lax.dynamic_update_slice(
        jnp.zeros_like(pivot),
        pivot_piece,
        (row * pivot_piece.shape[0], col * pivot_piece.shape[1]),
    )
    pivot = pivot + placed
    pivot = lax.all_to_all(
        pivot.reshape(n_pole * n_row, out_rows, width),
        ("pole", "row"),
        split_axis=0,
        concat_axis=0,
        tiled=True,
    )
    pivot = jnp.sum(pivot, 0)
    pivot = pivot + sum(shift(pivot, "col", d) for d in range(1, n_col))
    pivot = gather_all(pivot, ("pole", "row")).reshape(width, width)

    projected = dot(received, basis_super, ((1,), (0,)))
    charge = jnp.sum(ancestor * projected, 0)
    charge = charge + jnp.sum(basis_super * dot(pivot, basis_super, ((1,), (0,))), 0)
    return (upper_density, charge)


def solution(mesh):
    placed = (
        P("pole", None, "row", "col"),
        P("pole", None, "row", "col"),
        P("pole", None, "col", "row"),
        P("pole", None, "row", "col"),
        P("pole", None),
        P(),
        P(None, ("pole", "row", "col")),
        P(None, ("pole", "row", "col")),
    )
    return jax.shard_map(
        body,
        mesh=mesh,
        in_specs=placed,
        out_specs=(P(("pole", "row"), "col"), P(("pole", "row", "col"))),
        check_vma=False,
    )
```

```python
import jax
import jax.numpy as jnp
from jax import lax
from jax.experimental import pallas as pl
from jax.experimental.pallas import tpu as pltpu
from jax.sharding import PartitionSpec as P

BLOCKS = 18
HIGH = lax.Precision.HIGH
F32, BF16 = jnp.float32, jnp.bfloat16
LAST, INNER = ((1,), (1,)), ((1,), (0,))
SMEM = pl.BlockSpec(memory_space=pltpu.SMEM)
VMEM = pl.BlockSpec(memory_space=pltpu.VMEM)


def room(mebibytes):
    return pltpu.CompilerParams(vmem_limit_bytes=mebibytes * 2**20)


def halves(x):
    high = x.astype(BF16)
    return high, (x - high.astype(F32)).astype(BF16)


def product(left, right, contract):
    def one(a, b):
        return lax.dot_general(a, b, (contract, ((), ())), preferred_element_type=F32)

    return one(left[0], right[0]) + (one(left[0], right[1]) + one(left[1], right[0]))


QUICK = pl.CostEstimate(flops=0, bytes_accessed=0, transcendentals=0)


def fixed(shape):
    return pl.BlockSpec(shape, lambda i: (0,) * len(shape))


def lower_products(place, weights, tile, blocks, n_pole):
    _, _, rows, depth = tile.shape
    piece = blocks[0].shape[1]
    n_row = len(blocks)
    width = n_row * piece
    steps = 3
    chunk = rows // steps
    part = rows // n_pole

    def kernel(place, weights, tile, *refs):
        blocks, refs = refs[:n_row], refs[n_row:]
        outs, (out_h, out_l, right_h, right_l, whole) = refs[:n_pole], refs[n_pole:]
        step = pl.program_id(0)

        @pl.when(step == 0)
        def _():
            w_re, w_im = weights[0, 0], weights[0, 1]
            for d in range(n_row):
                re, im = blocks[d][0], blocks[d][1]
                re, im = w_re * re - w_im * im, w_re * im + w_im * re
                for side, pair in enumerate(((-im, -re), (re, -im))):
                    at = pl.multiple_of(side * width + (place[3] ^ d) * piece, 16)
                    for j, x in enumerate(pair):
                        cols = slice(j * depth, (j + 1) * depth)
                        right_h[pl.ds(at, piece), cols], right_l[pl.ds(at, piece), cols] = halves(x)

        left = halves(jnp.concatenate([tile[0, 0], tile[0, 1]], 1))
        out = product(left, (right_h[...], right_l[...]), LAST)
        out_h[...], out_l[...] = halves(out)
        whole[pl.ds(pl.multiple_of(step * chunk, 16), chunk), :] = out[:, :width]

        @pl.when(step == steps - 1)
        def _():
            for d in range(n_pole):
                at = pl.multiple_of((place[0] ^ d) * part, 8)
                outs[d][...] = whole[pl.ds(at, part), :]

    out = pl.pallas_call(
        kernel,
        grid=(steps,),
        in_specs=[SMEM, SMEM, pl.BlockSpec((1, 2, chunk, depth), lambda i: (0, 0, i, 0))]
        + [fixed(blocks[0].shape)] * n_row,
        out_specs=[fixed((part, width))] * n_pole + [pl.BlockSpec((chunk, 2 * width), lambda i: (i, 0))] * 2,
        out_shape=[jax.ShapeDtypeStruct((part, width), F32)] * n_pole
        + [jax.ShapeDtypeStruct((rows, 2 * width), BF16)] * 2,
        scratch_shapes=[pltpu.VMEM((2 * width, 2 * depth), BF16)] * 2 + [pltpu.VMEM((rows, width), F32)],
        compiler_params=room(58),
        cost_estimate=QUICK,
    )(place, weights, tile, *blocks)
    return out[:n_pole], out[n_pole:]


def pivot_term(place, weights, blocks, lower, pivot_inverse):
    rows = blocks[0].shape[0]
    n_col = len(blocks) // 2
    width = n_col * rows
    depth = lower[0].shape[0]
    piece_rows, piece_cols = pivot_inverse.shape[2:]

    def kernel(place, weights, *refs):
        blocks, (lower_h, lower_l, inverse, pivot, left_h, left_l) = refs[: 2 * n_col], refs[2 * n_col :]
        for p in range(n_col):
            at = pl.multiple_of(lax.rem(place[4] + p, n_col) * rows, 16)
            for j, x in enumerate((-blocks[2 * p][...], blocks[2 * p + 1][:, :depth])):
                at_j = slice(j * depth, (j + 1) * depth)
                left_h[pl.ds(at, rows), at_j], left_l[pl.ds(at, rows), at_j] = halves(x)
        right = [jnp.concatenate([x[:, :width], x[:, width:]], 0) for x in (lower_h, lower_l)]
        pivot[...] = product((left_h[...], left_l[...]), right, INNER)
        at = pl.multiple_of(place[3] * piece_rows, 8)
        own = weights[0, 0] * inverse[0, 1] + weights[0, 1] * inverse[0, 0]
        for k in range(n_col):

            @pl.when(place[4] == k)
            def _():
                pivot[pl.ds(at, piece_rows), k * piece_cols : (k + 1) * piece_cols] += own

    return pl.pallas_call(
        kernel,
        grid=(1,),
        in_specs=[SMEM, SMEM]
        + [fixed(x.shape) for x in blocks]
        + [fixed(lower[0].shape)] * 2
        + [fixed(pivot_inverse.shape)],
        out_specs=fixed((width, width)),
        out_shape=jax.ShapeDtypeStruct((width, width), F32),
        scratch_shapes=[pltpu.VMEM((width, 2 * depth), BF16)] * 2,
        compiler_params=room(58),
        cost_estimate=QUICK,
    )(place, weights, *blocks, *lower, pivot_inverse)


def upper_products(place, weights, tile, blocks):
    _, _, depth, cols = tile.shape
    rows = blocks[0].shape[0]
    n_col = len(blocks) // 2
    width = n_col * rows
    steps = 3
    chunk = depth // steps

    def kernel(place, weights, tile, *refs):
        blocks, refs = refs[: 2 * n_col], refs[2 * n_col :]
        upper, left_h, left_l = refs
        step = pl.program_id(0)
        w_re, w_im = weights[0, 0], weights[0, 1]

        def fill(combine):
            for p in range(n_col):
                at = pl.multiple_of(lax.rem(place[4] + p, n_col) * rows, 16)
                for j, x in enumerate(combine(blocks[2 * p][...], blocks[2 * p + 1][:, :depth])):
                    at_j = slice(j * depth, (j + 1) * depth)
                    left_h[pl.ds(at, rows), at_j], left_l[pl.ds(at, rows), at_j] = halves(x)

        @pl.when(step == 0)
        def _():
            fill(lambda re, im: (-(w_re * im + w_im * re), w_im * im - w_re * re))
            upper[...] = jnp.zeros_like(upper)

        right = halves(jnp.concatenate([tile[0, 0], tile[0, 1]], 0))
        at = [pl.ds(pl.multiple_of(j * depth + step * chunk, 128), chunk) for j in range(2)]
        left = [jnp.concatenate([ref[:, at[0]], ref[:, at[1]]], 1) for ref in (left_h, left_l)]
        upper[...] += product(left, right, INNER)

    return pl.pallas_call(
        kernel,
        grid=(steps,),
        in_specs=[SMEM, SMEM, pl.BlockSpec((1, 2, chunk, cols), lambda i: (0, 0, i, 0))]
        + [fixed(x.shape) for x in blocks],
        out_specs=fixed((width, cols)),
        out_shape=jax.ShapeDtypeStruct((width, cols), F32),
        scratch_shapes=[pltpu.VMEM((width, 2 * depth), BF16)] * 2,
        compiler_params=room(58),
        cost_estimate=QUICK,
    )(place, weights, tile, *blocks)


def routing(place, block_owners, n_pole, n_row, n_col, capacity):
    owners_here = n_row * n_col
    devices_all = n_pole * owners_here
    blocks, top = block_owners.shape
    lanes = -(-blocks // 128) * 128
    columns = -(-devices_all // 128) * 128

    def earlier(x, at, axis):
        count = jnp.zeros_like(x)
        for k in range(1, BLOCKS):
            count = count + jnp.where(at >= k, jnp.roll(x, k, axis), 0.0)
        return count

    def kernel(place, owners, slots, source):
        named = jnp.concatenate(
            [owners[...].astype(F32), jnp.full((top, lanes - blocks), -1.0, F32)], 1
        ) if lanes > blocks else owners[...].astype(F32)
        number = lax.broadcasted_iota(jnp.int32, (1, lanes), 1)
        within = lax.rem(number, BLOCKS)
        me = place[5].astype(F32)
        hit = jnp.zeros((1, lanes), F32)
        for t in range(top):
            hit = hit + jnp.where(named[t : t + 1] == me, 1.0, 0.0)
        rank = earlier(hit, within, 1)
        value = (within + 1).astype(F32) * hit
        by_slot = jnp.concatenate(
            [jnp.where(rank == s, value, 0.0) for s in range(capacity)]
            + [jnp.zeros((8 - capacity, lanes), F32)],
            0,
        )
        block = lax.broadcasted_iota(jnp.int32, (lanes, columns), 0)
        group = lax.broadcasted_iota(jnp.int32, (lanes, columns), 1)
        inside = jnp.where((block >= group * BLOCKS) & (block < (group + 1) * BLOCKS), 1.0, 0.0)
        slots[...] = jnp.dot(by_slot, inside, preferred_element_type=F32).astype(jnp.int32)
        block = lax.broadcasted_iota(jnp.int32, (lanes, 128), 0)
        at = lax.broadcasted_iota(jnp.int32, (lanes, 128), 1)
        owner = place[0] * owners_here + lax.broadcasted_iota(jnp.int32, (owners_here, 128), 0)
        local = lax.broadcasted_iota(jnp.int32, (owners_here, 128), 1)
        for d in range(n_pole):
            group = (place[3] * n_pole + (place[0] ^ d)) * n_col + place[4]
            own = jnp.where((block == group * BLOCKS + at) & (at < BLOCKS), 1.0, 0.0)
            here = jnp.dot(named + 1.0, own, preferred_element_type=F32) - 1.0
            hit = jnp.zeros((owners_here, 128), F32)
            for t in range(top):
                hit = hit + jnp.where(here[t : t + 1] == owner.astype(F32), 1.0, 0.0)
            rank = earlier(hit, local, 1)
            value = (local + 1).astype(F32) * hit
            out = jnp.zeros((owners_here, 128), F32)
            for s in range(capacity):
                total = jnp.sum(jnp.where(rank == s, value, 0.0), 1, keepdims=True)
                out = out + jnp.where(local == s, total, 0.0)
            source[d] = out.astype(jnp.int32)

    return pl.pallas_call(
        kernel,
        in_specs=[SMEM, VMEM],
        out_specs=[VMEM] * 2,
        out_shape=[
            jax.ShapeDtypeStruct((8, columns), jnp.int32),
            jax.ShapeDtypeStruct((n_pole, owners_here, 128), jnp.int32),
        ],
        cost_estimate=QUICK,
    )(place, block_owners.T)


def routed_blocks(place, slots, blocks, n_pole, n_row, n_col, capacity):
    _, rows, points = blocks.shape

    def kernel(place, slots, blocks, out):
        for row in range(n_row):
            for col in range(n_col):
                for d in range(n_pole):
                    group = (row * n_pole + (place[0] ^ d)) * n_col + col
                    for s in range(capacity):
                        at = jnp.maximum(slots[s, group] - 1, 0)
                        out[row * n_col + col, d * capacity + s] = blocks[group * BLOCKS + at]

    return pl.pallas_call(
        kernel,
        in_specs=[SMEM, SMEM, VMEM],
        out_specs=VMEM,
        out_shape=jax.ShapeDtypeStruct((n_row * n_col, n_pole * capacity, rows, points), F32),
        cost_estimate=QUICK,
    )(place, slots, blocks)


def charge_terms_plain(place, source, rows, pivots, bases, ancestor):
    n_pole, (n_rows, width) = len(rows), rows[0].shape
    n_row, owners, slots, block_rows, points = ancestor.shape
    capacity = slots // n_pole
    left = jnp.concatenate([sum(pivots)] + list(rows), 0)
    terms = []
    for at_row in range(n_row):
        basis = sum(jnp.where((place[3] ^ b) == at_row, x, 0.0) for b, x in bases.items())
        basis = jnp.roll(basis, place[4], 0)
        basis = basis.reshape(owners, basis.shape[1], -1, points).transpose(0, 2, 1, 3).reshape(owners, width, points)
        result = jnp.einsum("ij,kjg->kig", left, basis, precision=lax.Precision.HIGH)
        total = jnp.sum(result[:, :width] * basis, 1)
        blocks = result[:, width:].reshape(owners, n_pole * BLOCKS, block_rows, points)
        at = source[:, at_row * owners : (at_row + 1) * owners, :capacity].transpose(1, 0, 2) - 1
        place_of = jnp.maximum(at, 0) + jnp.arange(n_pole, dtype=jnp.int32)[None, :, None] * BLOCKS
        found = jax.vmap(lambda x, k: x[k])(blocks, place_of.reshape(owners, slots)) * ancestor[at_row]
        found = jnp.where(at.reshape(owners, slots, 1, 1) >= 0, found, 0.0)
        terms.append(total + jnp.sum(found, (1, 2)))
    return jnp.stack(terms)[:, :, None]


def charge_terms(place, source, rows, pivots, bases, ancestor):
    n_pole, (n_rows, width) = len(rows), rows[0].shape
    n_row, owners, slots, block_rows, points = ancestor.shape
    capacity = slots // n_pole
    fold = bases[0].shape[2] // points
    if block_rows % 8:
        return charge_terms_plain(place, source, rows, pivots, bases, ancestor)
    order = sorted(bases)
    n_groups = len(order)

    def kernel(place, source, *refs):
        rows, pivots, refs = refs[:n_pole], refs[n_pole : 2 * n_pole], refs[2 * n_pole :]
        ancestor, bases, (out, held) = refs[0], refs[1 : 1 + n_groups], refs[1 + n_groups :]
        pivot = pivots[0][...]
        for ref in pivots[1:]:
            pivot = pivot + ref[...]
        left = halves(jnp.concatenate([pivot] + [ref[...] for ref in rows], 0))
        for g, b in enumerate(order):
            at_row = place[3] ^ b
            basis = jnp.concatenate(
                [
                    jnp.concatenate([bases[g][k, :, f * points : (f + 1) * points] for f in range(fold)], 0)
                    for k in range(owners)
                ],
                1,
            )
            result = product(left, halves(basis), INNER)
            held[...] = result[width:]
            sums = jnp.sum(result[:width] * basis, 0, keepdims=True)
            for k in range(owners):
                o = lax.rem(place[4] + k, owners)
                lanes = slice(k * points, (k + 1) * points)
                found = jnp.zeros((block_rows, points), F32)
                for d in range(n_pole):
                    for s in range(capacity):
                        at = source[d, at_row * owners + o, s] - 1
                        first = pl.multiple_of(d * n_rows + jnp.maximum(at, 0) * block_rows, block_rows)
                        block = held[pl.ds(first, block_rows), lanes] * ancestor[at_row, o, d * capacity + s]
                        found = found + jnp.where(at >= 0, block, 0.0)
                out[at_row, o] = sums[:, lanes] + jnp.sum(found, 0, keepdims=True)

    return pl.pallas_call(
        kernel,
        in_specs=[SMEM, SMEM] + [VMEM] * (2 * n_pole + 1 + n_groups),
        out_specs=VMEM,
        out_shape=jax.ShapeDtypeStruct((n_row, owners, 1, points), F32),
        scratch_shapes=[pltpu.VMEM((n_pole * n_rows, owners * points), F32)],
        compiler_params=room(58),
        cost_estimate=QUICK,
    )(place, source, *rows, *pivots, ancestor, *[bases[k] for k in order])


def permute(x, axis, pairs):
    return lax.ppermute(x, axis, pairs)


def swap(x, axis, mask):
    return lax.ppermute(x, axis, [(i, i ^ mask) for i in range(lax.axis_size(axis))])


def shift(x, axis, by):
    n = lax.axis_size(axis)
    return lax.ppermute(x, axis, [(i, (i + by) % n) for i in range(n)])


def gather_swapped(x, axis, first):
    n = lax.axis_size(axis)
    held = {0: x}
    bit = n // 2
    while bit:
        for d in list(held):
            held[d ^ bit] = swap(after(held[d], *first) if d else x, axis, bit)
        bit //= 2
    return [held[d] for d in range(n)]


def gather_near(x, axis):
    n = lax.axis_size(axis)
    return [shift(x, axis, -p) for p in (range(1, n) if n != 4 else (1, 3))]


def gather_cyclic(x, near, axis):
    if lax.axis_size(axis) != 4:
        return [x] + near
    one, three = near
    leftward = permute(one, axis, [(2, 1), (1, 0)])
    rightward = permute(three, axis, [(1, 2), (2, 3)])
    return [x, one, (leftward, rightward), three]


def joined(blocks, axis, *ready):
    return [
        jnp.where(lax.axis_index(axis) < 2, after(x[0], *ready), x[1]) if isinstance(x, tuple) else x for x in blocks
    ]


def reduce_scatter_swapped(x, axis, masks):
    total = x[0]
    for term, mask in zip(x[1:], masks, strict=True):
        total = total + swap(term, axis, mask)
    return total


def pick(x, at):
    return lax.dynamic_index_in_dim(x, at, 0, keepdims=False)


def gather_all(x, axes):
    n = 1
    for axis in axes:
        n *= lax.axis_size(axis)
    spread = jnp.broadcast_to(x[None], (n,) + x.shape)
    return lax.all_to_all(spread, axes, split_axis=0, concat_axis=0, tiled=True)


def after(x, *others):
    return lax.optimization_barrier((x,) + others)[0]


def halving(x, axis, before, later):
    n = lax.axis_size(axis)
    me = lax.axis_index(axis)
    held = [pick(x, me ^ d) for d in range(n)]
    bit = 1
    while bit < n:
        away = [d for d in range(0, n, bit) if d & bit]
        out = jnp.stack([held[d] for d in away])
        if bit == 2:
            later = after(later, out)
        arrived = swap(out, axis, bit)
        if bit == 1:
            arrived = after(arrived, *before)
        for j, d in enumerate(away):
            held[d ^ bit] = held[d ^ bit] + arrived[j]
        bit *= 2
    return held[0], later


def body(
    inverse_tile,
    lower_factor,
    upper_factor,
    pivot_inverse,
    pole_weights,
    block_owners,
    basis_ancestor,
    basis_super,
):
    n_pole, n_row, n_col = (lax.axis_size(a) for a in ("pole", "row", "col"))
    pole, row, col = (lax.axis_index(a) for a in ("pole", "row", "col"))
    devices_all = n_pole * n_row * n_col
    tile_rows, tile_cols = inverse_tile.shape[2:]
    width, points = basis_super.shape
    capacity = max(2, (BLOCKS * block_owners.shape[1] + devices_all - 1) // devices_all)
    piece = upper_factor.shape[2]
    rows_here = tile_rows // (n_pole * n_col)
    block_rows = rows_here // BLOCKS
    out_rows = width // (n_pole * n_row)
    groups = n_row * n_pole * n_col
    me = (pole * n_row + row) * n_col + col
    position = (row * n_pole + pole) * n_col + col
    place = jnp.stack([pole, row // 2, row % 2, row, col, me, position]).astype(jnp.int32)

    fold = width // piece
    basis = basis_super.reshape(fold, piece, points).transpose(1, 0, 2).reshape(piece, fold * points)
    upper_own = [upper_factor[0, 0], jnp.concatenate([upper_factor[0, 1], basis], 1)]
    upper_near = [gather_near(x, "col") for x in upper_own]

    slots, source = routing(place, block_owners, n_pole, n_row, n_col, capacity)
    ancestor = routed_blocks(
        place, slots, basis_ancestor.reshape(groups * BLOCKS, block_rows, points), n_pole, n_row, n_col, capacity
    )
    lower = gather_swapped(lower_factor[0], "row", (ancestor, *upper_near[0]))


    parts, beside = lower_products(place, pole_weights, inverse_tile, lower, n_pole)
    upper = [
        gather_cyclic(upper_own[0], upper_near[0], "col"),
        gather_cyclic(upper_own[1], [after(x, parts[0]) for x in upper_near[1]], "col"),
    ]
    half = reduce_scatter_swapped(parts, "pole", list(range(1, n_pole)))
    upper[1] = joined(upper[1], "col")
    ancestor = lax.all_to_all(
        after(ancestor, upper[1][n_col // 2]), ("row", "col"), split_axis=0, concat_axis=0, tiled=True
    ).reshape(n_row, n_col, -1, block_rows, points)

    line = jnp.stack([x[:, tile_rows:] for x in upper[1]])
    bases = {b: swap(line, "row", b) if b else line for b in range(0, n_row, 2)}
    upper[0] = joined(upper[0], "col", half)
    upper = [x for pair in zip(*upper, strict=True) for x in pair]

    pivot = pivot_term(place, pole_weights, upper, beside, pivot_inverse)
    pivots = [pivot] + [swap(pivot, "pole", d) for d in range(1, n_pole)]
    product_upper = upper_products(place, after(pole_weights, pivot), inverse_tile, upper)
    for b in list(bases):
        bases[b + 1] = swap(bases[b], "row", 1)
    rows, product_upper = halving(half.reshape(n_col, rows_here, width), "col", (product_upper, pivots[-1]), product_upper)
    rows = [rows] + [swap(rows, "pole", d) for d in range(1, n_pole)]
    arrived = lax.all_to_all(
        product_upper.reshape(n_pole * n_row, -1, tile_cols),
        ("pole", "row"),
        split_axis=0,
        concat_axis=0,
        tiled=True,
    )

    terms = charge_terms(place, source, rows, pivots, bases, ancestor)
    terms = lax.all_to_all(
        after(terms, arrived).reshape(n_row * n_col, 1, points),
        ("row", "col"),
        split_axis=0,
        concat_axis=0,
        tiled=True,
    )
    return (jnp.sum(arrived, 0), jnp.sum(terms, (0, 1)))


def solution(mesh):
    placed = (
        P("pole", None, "row", "col"),
        P("pole", None, "row", "col"),
        P("pole", None, "col", "row"),
        P("pole", None, "row", "col"),
        P("pole", None),
        P(),
        P(None, ("pole", "row", "col")),
        P(None, ("pole", "row", "col")),
    )
    return jax.shard_map(
        body,
        mesh=mesh,
        in_specs=placed,
        out_specs=(P(("pole", "row"), "col"), P(("pole", "row", "col"))),
        check_vma=False,
    )
```

```python
import jax
import jax.numpy as jnp
from jax import lax
from jax.experimental import pallas as pl
from jax.experimental.pallas import tpu as pltpu
from jax.sharding import PartitionSpec as P

BLOCKS = 18
HIGH = lax.Precision.HIGH
F32, BF16 = jnp.float32, jnp.bfloat16
LAST, INNER = ((1,), (1,)), ((1,), (0,))
SMEM = pl.BlockSpec(memory_space=pltpu.SMEM)
VMEM = pl.BlockSpec(memory_space=pltpu.VMEM)


def room(mebibytes):
    return pltpu.CompilerParams(vmem_limit_bytes=mebibytes * 2**20)


def halves(x):
    high = x.astype(BF16)
    return high, (x - high.astype(F32)).astype(BF16)


def product(left, right, contract):
    def one(a, b):
        return lax.dot_general(a, b, (contract, ((), ())), preferred_element_type=F32)

    return one(left[0], right[0]) + (one(left[0], right[1]) + one(left[1], right[0]))


QUICK = pl.CostEstimate(flops=0, bytes_accessed=0, transcendentals=0)


def fixed(shape):
    return pl.BlockSpec(shape, lambda i: (0,) * len(shape))


def lower_products(place, weights, tile, blocks, n_pole):
    _, _, rows, depth = tile.shape
    piece = blocks[0].shape[1]
    n_row = len(blocks)
    width = n_row * piece
    steps = 3
    chunk = rows // steps
    part = rows // n_pole

    def kernel(place, weights, tile, *refs):
        blocks, refs = refs[:n_row], refs[n_row:]
        outs, (out_h, out_l, right_h, right_l, whole) = refs[:n_pole], refs[n_pole:]
        step = pl.program_id(0)

        @pl.when(step == 0)
        def _():
            w_re, w_im = weights[0, 0], weights[0, 1]
            for d in range(n_row):
                re, im = blocks[d][0], blocks[d][1]
                re, im = w_re * re - w_im * im, w_re * im + w_im * re
                for side, pair in enumerate(((-im, -re), (re, -im))):
                    at = pl.multiple_of(side * width + (place[3] ^ d) * piece, 16)
                    for j, x in enumerate(pair):
                        cols = slice(j * depth, (j + 1) * depth)
                        right_h[pl.ds(at, piece), cols], right_l[pl.ds(at, piece), cols] = halves(x)

        left = halves(jnp.concatenate([tile[0, 0], tile[0, 1]], 1))
        out = product(left, (right_h[...], right_l[...]), LAST)
        out_h[...], out_l[...] = halves(out)
        whole[pl.ds(pl.multiple_of(step * chunk, 16), chunk), :] = out[:, :width]

        @pl.when(step == steps - 1)
        def _():
            for d in range(n_pole):
                at = pl.multiple_of((place[0] ^ d) * part, 8)
                outs[d][...] = whole[pl.ds(at, part), :]

    out = pl.pallas_call(
        kernel,
        grid=(steps,),
        in_specs=[SMEM, SMEM, pl.BlockSpec((1, 2, chunk, depth), lambda i: (0, 0, i, 0))]
        + [fixed(blocks[0].shape)] * n_row,
        out_specs=[fixed((part, width))] * n_pole + [pl.BlockSpec((chunk, 2 * width), lambda i: (i, 0))] * 2,
        out_shape=[jax.ShapeDtypeStruct((part, width), F32)] * n_pole
        + [jax.ShapeDtypeStruct((rows, 2 * width), BF16)] * 2,
        scratch_shapes=[pltpu.VMEM((2 * width, 2 * depth), BF16)] * 2 + [pltpu.VMEM((rows, width), F32)],
        compiler_params=room(58),
        cost_estimate=QUICK,
    )(place, weights, tile, *blocks)
    return out[:n_pole], out[n_pole:]


def flattened(blocks):
    pairs = [x if isinstance(x, tuple) else (x,) for x in blocks]
    return [y for x in pairs for y in x], [len(x) for x in pairs]


def loaded(refs, counts, col, depth):
    out, at = [], 0
    for count in counts:
        x = refs[at][:, :depth]
        out.append(x if count == 1 else jnp.where(col < 2, x, refs[at + 1][:, :depth]))
        at += count
    return out


def pivot_term(place, weights, blocks, lower, pivot_inverse):
    rows = blocks[0].shape[0]
    n_col = len(blocks) // 2
    flat, counts = flattened(blocks)
    width = n_col * rows
    depth = lower[0].shape[0]
    piece_rows, piece_cols = pivot_inverse.shape[2:]

    def kernel(place, weights, *refs):
        blocks, refs = refs[: len(flat)], refs[len(flat) :]
        lower_h, lower_l, inverse, pivot, left_h, left_l = refs
        blocks = loaded(blocks, counts, place[4], depth)
        for p in range(n_col):
            at = pl.multiple_of(lax.rem(place[4] + p, n_col) * rows, 16)
            for j, x in enumerate((-blocks[2 * p], blocks[2 * p + 1])):
                at_j = slice(j * depth, (j + 1) * depth)
                left_h[pl.ds(at, rows), at_j], left_l[pl.ds(at, rows), at_j] = halves(x)
        right = [jnp.concatenate([x[:, :width], x[:, width:]], 0) for x in (lower_h, lower_l)]
        pivot[...] = product((left_h[...], left_l[...]), right, INNER)
        at = pl.multiple_of(place[3] * piece_rows, 8)
        own = weights[0, 0] * inverse[0, 1] + weights[0, 1] * inverse[0, 0]
        for k in range(n_col):

            @pl.when(place[4] == k)
            def _():
                pivot[pl.ds(at, piece_rows), k * piece_cols : (k + 1) * piece_cols] += own

    return pl.pallas_call(
        kernel,
        grid=(1,),
        in_specs=[SMEM, SMEM]
        + [fixed(x.shape) for x in flat]
        + [fixed(lower[0].shape)] * 2
        + [fixed(pivot_inverse.shape)],
        out_specs=fixed((width, width)),
        out_shape=jax.ShapeDtypeStruct((width, width), F32),
        scratch_shapes=[pltpu.VMEM((width, 2 * depth), BF16)] * 2,
        compiler_params=room(58),
        cost_estimate=QUICK,
    )(place, weights, *flat, *lower, pivot_inverse)


def upper_products(place, weights, tile, blocks, n_groups):
    _, _, depth, cols = tile.shape
    rows = blocks[0].shape[0]
    n_col = len(blocks) // 2
    flat, counts = flattened(blocks)
    width = n_col * rows
    steps = 3
    chunk = depth // steps

    def kernel(place, weights, tile, *refs):
        blocks, refs = refs[: len(flat)], refs[len(flat) :]
        keep, send, left_h, left_l, upper = refs
        step = pl.program_id(0)
        w_re, w_im = weights[0, 0], weights[0, 1]

        def fill(combine):
            held = loaded(blocks, counts, place[4], depth)
            for p in range(n_col):
                at = pl.multiple_of(lax.rem(place[4] + p, n_col) * rows, 16)
                for j, x in enumerate(combine(held[2 * p], held[2 * p + 1])):
                    at_j = slice(j * depth, (j + 1) * depth)
                    left_h[pl.ds(at, rows), at_j], left_l[pl.ds(at, rows), at_j] = halves(x)

        @pl.when(step == 0)
        def _():
            fill(lambda re, im: (-(w_re * im + w_im * re), w_im * im - w_re * re))
            upper[...] = jnp.zeros_like(upper)

        right = halves(jnp.concatenate([tile[0, 0], tile[0, 1]], 0))
        at = [pl.ds(pl.multiple_of(j * depth + step * chunk, 128), chunk) for j in range(2)]
        left = [jnp.concatenate([ref[:, at[0]], ref[:, at[1]]], 1) for ref in (left_h, left_l)]
        total = upper[...] + product(left, right, INNER)
        upper[...] = total

        @pl.when(step == steps - 1)
        def _():
            pairs = total.reshape(n_groups // 2, 2, width // n_groups, cols)
            keep[...] = jnp.where(place[2] == 0, pairs[:, 0], pairs[:, 1])
            send[...] = jnp.where(place[2] == 0, pairs[:, 1], pairs[:, 0])

    part = (n_groups // 2, width // n_groups, cols)

    return pl.pallas_call(
        kernel,
        grid=(steps,),
        in_specs=[SMEM, SMEM, pl.BlockSpec((1, 2, chunk, cols), lambda i: (0, 0, i, 0))]
        + [fixed(x.shape) for x in flat],
        out_specs=[fixed(part)] * 2,
        out_shape=[jax.ShapeDtypeStruct(part, F32)] * 2,
        scratch_shapes=[pltpu.VMEM((width, 2 * depth), BF16)] * 2 + [pltpu.VMEM((width, cols), F32)],
        compiler_params=room(58),
        cost_estimate=QUICK,
    )(place, weights, tile, *flat)


def routing(place, block_owners, n_pole, n_row, n_col, capacity):
    owners_here = n_row * n_col
    devices_all = n_pole * owners_here
    blocks, top = block_owners.shape
    lanes = -(-blocks // 128) * 128
    columns = -(-devices_all // 128) * 128

    def earlier(x, at, axis):
        count = jnp.zeros_like(x)
        for k in range(1, BLOCKS):
            count = count + jnp.where(at >= k, jnp.roll(x, k, axis), 0.0)
        return count

    def kernel(place, owners, slots, source):
        named = jnp.concatenate(
            [owners[...].astype(F32), jnp.full((top, lanes - blocks), -1.0, F32)], 1
        ) if lanes > blocks else owners[...].astype(F32)
        number = lax.broadcasted_iota(jnp.int32, (1, lanes), 1)
        within = lax.rem(number, BLOCKS)
        me = place[5].astype(F32)
        hit = jnp.zeros((1, lanes), F32)
        for t in range(top):
            hit = hit + jnp.where(named[t : t + 1] == me, 1.0, 0.0)
        rank = earlier(hit, within, 1)
        value = (within + 1).astype(F32) * hit
        by_slot = jnp.concatenate(
            [jnp.where(rank == s, value, 0.0) for s in range(capacity)]
            + [jnp.zeros((8 - capacity, lanes), F32)],
            0,
        )
        block = lax.broadcasted_iota(jnp.int32, (lanes, columns), 0)
        group = lax.broadcasted_iota(jnp.int32, (lanes, columns), 1)
        inside = jnp.where((block >= group * BLOCKS) & (block < (group + 1) * BLOCKS), 1.0, 0.0)
        slots[...] = jnp.dot(by_slot, inside, preferred_element_type=F32).astype(jnp.int32)
        block = lax.broadcasted_iota(jnp.int32, (lanes, 128), 0)
        at = lax.broadcasted_iota(jnp.int32, (lanes, 128), 1)
        owner = place[0] * owners_here + lax.broadcasted_iota(jnp.int32, (owners_here, 128), 0)
        local = lax.broadcasted_iota(jnp.int32, (owners_here, 128), 1)
        for d in range(n_pole):
            group = (place[3] * n_pole + (place[0] ^ d)) * n_col + place[4]
            own = jnp.where((block == group * BLOCKS + at) & (at < BLOCKS), 1.0, 0.0)
            here = jnp.dot(named + 1.0, own, preferred_element_type=F32) - 1.0
            hit = jnp.zeros((owners_here, 128), F32)
            for t in range(top):
                hit = hit + jnp.where(here[t : t + 1] == owner.astype(F32), 1.0, 0.0)
            rank = earlier(hit, local, 1)
            value = (local + 1).astype(F32) * hit
            out = jnp.zeros((owners_here, 128), F32)
            for s in range(capacity):
                total = jnp.sum(jnp.where(rank == s, value, 0.0), 1, keepdims=True)
                out = out + jnp.where(local == s, total, 0.0)
            source[d] = out.astype(jnp.int32)

    return pl.pallas_call(
        kernel,
        in_specs=[SMEM, VMEM],
        out_specs=[VMEM] * 2,
        out_shape=[
            jax.ShapeDtypeStruct((8, columns), jnp.int32),
            jax.ShapeDtypeStruct((n_pole, owners_here, 128), jnp.int32),
        ],
        cost_estimate=QUICK,
    )(place, block_owners.T)


def routed_blocks(place, slots, blocks, n_pole, n_row, n_col, capacity):
    _, rows, points = blocks.shape

    def kernel(place, slots, blocks, out):
        for row in range(n_row):
            for col in range(n_col):
                for d in range(n_pole):
                    group = (row * n_pole + (place[0] ^ d)) * n_col + col
                    for s in range(capacity):
                        at = jnp.maximum(slots[s, group] - 1, 0)
                        out[row * n_col + col, d * capacity + s] = blocks[group * BLOCKS + at]

    return pl.pallas_call(
        kernel,
        in_specs=[SMEM, SMEM, VMEM],
        out_specs=VMEM,
        out_shape=jax.ShapeDtypeStruct((n_row * n_col, n_pole * capacity, rows, points), F32),
        cost_estimate=QUICK,
    )(place, slots, blocks)


def charge_terms_plain(place, source, rows, pivots, bases, ancestor):
    n_pole, (n_rows, width) = len(rows), rows[0][0].shape
    n_row, owners, slots, block_rows, points = ancestor.shape
    capacity = slots // n_pole
    left = jnp.concatenate([sum(pivots)] + [sum(x) for x in rows], 0)
    terms = []
    for at_row in range(n_row):
        basis = sum(jnp.where((place[3] ^ b) == at_row, x, 0.0) for b, x in bases.items())
        basis = jnp.roll(basis, place[4], 0)
        basis = basis.reshape(owners, basis.shape[1], -1, points).transpose(0, 2, 1, 3).reshape(owners, width, points)
        result = jnp.einsum("ij,kjg->kig", left, basis, precision=lax.Precision.HIGH)
        total = jnp.sum(result[:, :width] * basis, 1)
        blocks = result[:, width:].reshape(owners, n_pole * BLOCKS, block_rows, points)
        at = source[:, at_row * owners : (at_row + 1) * owners, :capacity].transpose(1, 0, 2) - 1
        place_of = jnp.maximum(at, 0) + jnp.arange(n_pole, dtype=jnp.int32)[None, :, None] * BLOCKS
        found = jax.vmap(lambda x, k: x[k])(blocks, place_of.reshape(owners, slots)) * ancestor[at_row]
        found = jnp.where(at.reshape(owners, slots, 1, 1) >= 0, found, 0.0)
        terms.append(total + jnp.sum(found, (1, 2)))
    return jnp.stack(terms)[:, :, None]


def charge_terms(place, source, rows, pivots, bases, ancestor):
    n_pole, (n_rows, width) = len(rows), rows[0][0].shape
    n_row, owners, slots, block_rows, points = ancestor.shape
    capacity = slots // n_pole
    n_terms = len(rows[0])
    fold = bases[0].shape[2] // points
    if block_rows % 8:
        return charge_terms_plain(place, source, rows, pivots, bases, ancestor)
    order = sorted(bases)
    n_groups = len(order)

    def kernel(place, source, *refs):
        rows, pivots, refs = refs[: n_pole * n_terms], refs[n_pole * n_terms :][:n_pole], refs[n_pole * (n_terms + 1) :]
        rows = [sum(ref[...] for ref in rows[d * n_terms : (d + 1) * n_terms]) for d in range(n_pole)]
        ancestor, bases, (out, held) = refs[0], refs[1 : 1 + n_groups], refs[1 + n_groups :]
        pivot = pivots[0][...]
        for ref in pivots[1:]:
            pivot = pivot + ref[...]
        left = halves(jnp.concatenate([pivot] + rows, 0))
        for g, b in enumerate(order):
            at_row = place[3] ^ b
            basis = jnp.concatenate(
                [
                    jnp.concatenate([bases[g][k, :, f * points : (f + 1) * points] for f in range(fold)], 0)
                    for k in range(owners)
                ],
                1,
            )
            result = product(left, halves(basis), INNER)
            held[...] = result[width:]
            sums = jnp.sum(result[:width] * basis, 0, keepdims=True)
            for k in range(owners):
                o = lax.rem(place[4] + k, owners)
                lanes = slice(k * points, (k + 1) * points)
                found = jnp.zeros((block_rows, points), F32)
                for d in range(n_pole):
                    for s in range(capacity):
                        at = source[d, at_row * owners + o, s] - 1
                        first = pl.multiple_of(d * n_rows + jnp.maximum(at, 0) * block_rows, block_rows)
                        block = held[pl.ds(first, block_rows), lanes] * ancestor[at_row, o, d * capacity + s]
                        found = found + jnp.where(at >= 0, block, 0.0)
                out[at_row, o] = sums[:, lanes] + jnp.sum(found, 0, keepdims=True)

    return pl.pallas_call(
        kernel,
        in_specs=[SMEM, SMEM] + [VMEM] * (n_pole * (n_terms + 1) + 1 + n_groups),
        out_specs=VMEM,
        out_shape=jax.ShapeDtypeStruct((n_row, owners, 1, points), F32),
        scratch_shapes=[pltpu.VMEM((n_pole * n_rows, owners * points), F32)],
        compiler_params=room(58),
        cost_estimate=QUICK,
    )(place, source, *[x for terms in rows for x in terms], *pivots, ancestor, *[bases[k] for k in order])


def permute(x, axis, pairs):
    return lax.ppermute(x, axis, pairs)


def swap(x, axis, mask):
    return lax.ppermute(x, axis, [(i, i ^ mask) for i in range(lax.axis_size(axis))])


def shift(x, axis, by):
    n = lax.axis_size(axis)
    return lax.ppermute(x, axis, [(i, (i + by) % n) for i in range(n)])


def gather_swapped(x, axis, first):
    n = lax.axis_size(axis)
    held = {0: x}
    bit = n // 2
    while bit:
        for d in list(held):
            held[d ^ bit] = swap(after(held[d], *first) if d else x, axis, bit)
        bit //= 2
    return [held[d] for d in range(n)]


def gather_near(x, axis):
    n = lax.axis_size(axis)
    return [shift(x, axis, -p) for p in (range(1, n) if n != 4 else (1, 3))]


def gather_cyclic(x, near, axis):
    if lax.axis_size(axis) != 4:
        return [x] + near
    one, three = near
    leftward = permute(one, axis, [(2, 1), (1, 0)])
    rightward = permute(three, axis, [(1, 2), (2, 3)])
    return [x, one, (leftward, rightward), three]


def joined(blocks, axis):
    return [jnp.where(lax.axis_index(axis) < 2, x[0], x[1]) if isinstance(x, tuple) else x for x in blocks]


def reduce_scatter_swapped(x, axis, masks):
    total = x[0]
    for term, mask in zip(x[1:], masks, strict=True):
        total = total + swap(term, axis, mask)
    return total


def pick(x, at):
    return lax.dynamic_index_in_dim(x, at, 0, keepdims=False)


def gather_all(x, axes):
    n = 1
    for axis in axes:
        n *= lax.axis_size(axis)
    spread = jnp.broadcast_to(x[None], (n,) + x.shape)
    return lax.all_to_all(spread, axes, split_axis=0, concat_axis=0, tiled=True)


def after(x, *others):
    return lax.optimization_barrier((x,) + others)[0]


def swap_both(x, axes, masks):
    first, second = (lax.axis_size(a) for a in axes)
    pairs = [
        (i * second + j, (i ^ masks[0]) * second + (j ^ masks[1])) for i in range(first) for j in range(second)
    ]
    return lax.ppermute(x, axes, pairs)


def rows_by_pole(x, before, later):
    n_pole, n_col = lax.axis_size("pole"), lax.axis_size("col")
    me = lax.axis_index("col")
    held = [pick(x, me ^ d) for d in range(n_col)]
    bit = 1
    while bit < n_col:
        away = [d for d in range(0, n_col, bit) if d & bit]
        if bit == 2 and n_col == 4:
            mine, other = held[0], held[2]
            later = after(later, other)
            rows = [[mine, swap(other, "col", 2)]]
            for d in range(1, n_pole):
                rows.append([swap(mine, "pole", d), swap_both(other, ("pole", "col"), (d, 2))])
            return rows, later
        arrived = swap(jnp.stack([held[d] for d in away]), "col", bit)
        if bit == 1:
            arrived = after(arrived, *before)
        for j, d in enumerate(away):
            held[d ^ bit] = held[d ^ bit] + arrived[j]
        bit *= 2
    return [[held[0]]] + [[swap(held[0], "pole", d)] for d in range(1, n_pole)], later


def body(
    inverse_tile,
    lower_factor,
    upper_factor,
    pivot_inverse,
    pole_weights,
    block_owners,
    basis_ancestor,
    basis_super,
):
    n_pole, n_row, n_col = (lax.axis_size(a) for a in ("pole", "row", "col"))
    pole, row, col = (lax.axis_index(a) for a in ("pole", "row", "col"))
    devices_all = n_pole * n_row * n_col
    tile_rows, tile_cols = inverse_tile.shape[2:]
    width, points = basis_super.shape
    capacity = max(2, (BLOCKS * block_owners.shape[1] + devices_all - 1) // devices_all)
    piece = upper_factor.shape[2]
    rows_here = tile_rows // (n_pole * n_col)
    block_rows = rows_here // BLOCKS
    out_rows = width // (n_pole * n_row)
    groups = n_row * n_pole * n_col
    me = (pole * n_row + row) * n_col + col
    position = (row * n_pole + pole) * n_col + col
    place = jnp.stack([pole, row // 2, row % 2, row, col, me, position]).astype(jnp.int32)

    fold = width // piece
    basis = basis_super.reshape(fold, piece, points).transpose(1, 0, 2).reshape(piece, fold * points)
    upper_own = [upper_factor[0, 0], jnp.concatenate([upper_factor[0, 1], basis], 1)]
    upper_near = [gather_near(x, "col") for x in upper_own]

    slots, source = routing(place, block_owners, n_pole, n_row, n_col, capacity)
    ancestor = routed_blocks(
        place, slots, basis_ancestor.reshape(groups * BLOCKS, block_rows, points), n_pole, n_row, n_col, capacity
    )
    lower = gather_swapped(lower_factor[0], "row", (ancestor, *upper_near[0]))


    parts, beside = lower_products(place, pole_weights, inverse_tile, lower, n_pole)
    upper = [
        gather_cyclic(upper_own[0], upper_near[0], "col"),
        gather_cyclic(upper_own[1], [after(x, parts[0]) for x in upper_near[1]], "col"),
    ]
    ancestor = lax.all_to_all(
        after(ancestor, parts[0], upper_near[1][-1]), ("row", "col"), split_axis=0, concat_axis=0, tiled=True
    ).reshape(n_row, n_col, -1, block_rows, points)
    half = reduce_scatter_swapped(parts, "pole", list(range(1, n_pole)))

    line = jnp.stack(joined([jax.tree.map(lambda y: y[:, tile_rows:], x) for x in upper[1]], "col"))
    bases = {b: swap(line, "row", b) if b else line for b in range(0, n_row, 2)}
    upper = [x for pair in zip(*upper, strict=True) for x in pair]

    pivot = pivot_term(place, pole_weights, upper, beside, after(pivot_inverse, half))
    pivots = [pivot] + [swap(pivot, "pole", d) for d in range(1, n_pole)]
    keep, send = upper_products(place, after(pole_weights, pivot), inverse_tile, upper, n_pole * n_row)
    for b in list(bases):
        bases[b + 1] = swap(bases[b], "row", 1)
    rows, send = rows_by_pole(half.reshape(n_col, rows_here, width), (keep,), send)
    near = (keep + swap(send, "row", 1)).reshape(n_pole, n_row // 2, -1, tile_cols)
    upper_density, arrived = 0.0, []
    for a in range(n_pole):
        for b in range(n_row // 2):
            part = pick(pick(near, pole ^ a), (row // 2) ^ b)
            if a or b:
                arrived.append(swap_both(part, ("pole", "row"), (a, 2 * b)))
            else:
                upper_density = part

    terms = charge_terms(place, source, rows, pivots, bases, ancestor)
    terms = lax.all_to_all(
        after(terms, *arrived).reshape(n_row * n_col, 1, points),
        ("row", "col"),
        split_axis=0,
        concat_axis=0,
        tiled=True,
    )
    return (upper_density + sum(arrived), jnp.sum(terms, (0, 1)))


def solution(mesh):
    placed = (
        P("pole", None, "row", "col"),
        P("pole", None, "row", "col"),
        P("pole", None, "col", "row"),
        P("pole", None, "row", "col"),
        P("pole", None),
        P(),
        P(None, ("pole", "row", "col")),
        P(None, ("pole", "row", "col")),
    )
    return jax.shard_map(
        body,
        mesh=mesh,
        in_specs=placed,
        out_specs=(P(("pole", "row"), "col"), P(("pole", "row", "col"))),
        check_vma=False,
    )
```

```python
import jax
import jax.numpy as jnp
from jax import lax
from jax.experimental import pallas as pl
from jax.experimental.pallas import tpu as pltpu
from jax.sharding import PartitionSpec as P

BLOCKS = 18
HIGH = lax.Precision.HIGH
F32, BF16 = jnp.float32, jnp.bfloat16
LAST, INNER = ((1,), (1,)), ((1,), (0,))
SMEM = pl.BlockSpec(memory_space=pltpu.SMEM)
VMEM = pl.BlockSpec(memory_space=pltpu.VMEM)


def room(mebibytes):
    return pltpu.CompilerParams(vmem_limit_bytes=mebibytes * 2**20)


def halves(x):
    high = x.astype(BF16)
    return high, (x - high.astype(F32)).astype(BF16)


def product(left, right, contract):
    def one(a, b):
        return lax.dot_general(a, b, (contract, ((), ())), preferred_element_type=F32)

    return one(left[0], right[0]) + (one(left[0], right[1]) + one(left[1], right[0]))


QUICK = pl.CostEstimate(flops=0, bytes_accessed=0, transcendentals=0)


def fixed(shape):
    return pl.BlockSpec(shape, lambda i: (0,) * len(shape))


def lower_products(place, weights, tile, blocks, n_pole):
    _, _, rows, depth = tile.shape
    piece = blocks[0].shape[1]
    n_row = len(blocks)
    width = n_row * piece
    steps = 3
    chunk = rows // steps
    part = rows // n_pole

    def kernel(place, weights, tile, *refs):
        blocks, refs = refs[:n_row], refs[n_row:]
        outs, (out_h, out_l, right_h, right_l, whole) = refs[:n_pole], refs[n_pole:]
        step = pl.program_id(0)

        @pl.when(step == 0)
        def _():
            w_re, w_im = weights[0, 0], weights[0, 1]
            for d in range(n_row):
                re, im = blocks[d][0], blocks[d][1]
                re, im = w_re * re - w_im * im, w_re * im + w_im * re
                for side, pair in enumerate(((-im, -re), (re, -im))):
                    at = pl.multiple_of(side * width + (place[3] ^ d) * piece, 16)
                    for j, x in enumerate(pair):
                        cols = slice(j * depth, (j + 1) * depth)
                        right_h[pl.ds(at, piece), cols], right_l[pl.ds(at, piece), cols] = halves(x)

        left = halves(jnp.concatenate([tile[0, 0], tile[0, 1]], 1))
        out = product(left, (right_h[...], right_l[...]), LAST)
        out_h[...], out_l[...] = halves(out)
        whole[pl.ds(pl.multiple_of(step * chunk, 16), chunk), :] = out[:, :width]

        @pl.when(step == steps - 1)
        def _():
            for d in range(n_pole):
                at = pl.multiple_of((place[0] ^ d) * part, 8)
                outs[d][...] = whole[pl.ds(at, part), :]

    out = pl.pallas_call(
        kernel,
        grid=(steps,),
        in_specs=[SMEM, SMEM, pl.BlockSpec((1, 2, chunk, depth), lambda i: (0, 0, i, 0))]
        + [fixed(blocks[0].shape)] * n_row,
        out_specs=[fixed((part, width))] * n_pole + [pl.BlockSpec((chunk, 2 * width), lambda i: (i, 0))] * 2,
        out_shape=[jax.ShapeDtypeStruct((part, width), F32)] * n_pole
        + [jax.ShapeDtypeStruct((rows, 2 * width), BF16)] * 2,
        scratch_shapes=[pltpu.VMEM((2 * width, 2 * depth), BF16)] * 2 + [pltpu.VMEM((rows, width), F32)],
        compiler_params=room(58),
        cost_estimate=QUICK,
    )(place, weights, tile, *blocks)
    return out[:n_pole], out[n_pole:]


def flattened(blocks):
    pairs = [x if isinstance(x, tuple) else (x,) for x in blocks]
    return [y for x in pairs for y in x], [len(x) for x in pairs]


def loaded(refs, counts, col, depth):
    out, at = [], 0
    for count in counts:
        x = refs[at][:, :depth]
        out.append(x if count == 1 else jnp.where(col < 2, x, refs[at + 1][:, :depth]))
        at += count
    return out


def pivot_term(place, weights, blocks, lower, pivot_inverse):
    rows = blocks[0].shape[0]
    n_col = len(blocks) // 2
    flat, counts = flattened(blocks)
    width = n_col * rows
    depth = lower[0].shape[0]
    piece_rows, piece_cols = pivot_inverse.shape[2:]

    def kernel(place, weights, *refs):
        blocks, refs = refs[: len(flat)], refs[len(flat) :]
        lower_h, lower_l, inverse, pivot, left_h, left_l = refs
        blocks = loaded(blocks, counts, place[4], depth)
        for p in range(n_col):
            at = pl.multiple_of(lax.rem(place[4] + p, n_col) * rows, 16)
            for j, x in enumerate((-blocks[2 * p], blocks[2 * p + 1])):
                at_j = slice(j * depth, (j + 1) * depth)
                left_h[pl.ds(at, rows), at_j], left_l[pl.ds(at, rows), at_j] = halves(x)
        right = [jnp.concatenate([x[:, :width], x[:, width:]], 0) for x in (lower_h, lower_l)]
        pivot[...] = product((left_h[...], left_l[...]), right, INNER)
        at = pl.multiple_of(place[3] * piece_rows, 8)
        own = weights[0, 0] * inverse[0, 1] + weights[0, 1] * inverse[0, 0]
        for k in range(n_col):

            @pl.when(place[4] == k)
            def _():
                pivot[pl.ds(at, piece_rows), k * piece_cols : (k + 1) * piece_cols] += own

    return pl.pallas_call(
        kernel,
        grid=(1,),
        in_specs=[SMEM, SMEM]
        + [fixed(x.shape) for x in flat]
        + [fixed(lower[0].shape)] * 2
        + [fixed(pivot_inverse.shape)],
        out_specs=fixed((width, width)),
        out_shape=jax.ShapeDtypeStruct((width, width), F32),
        scratch_shapes=[pltpu.VMEM((width, 2 * depth), BF16)] * 2,
        compiler_params=room(24),
        cost_estimate=QUICK,
    )(place, weights, *flat, *lower, pivot_inverse)


def upper_products(place, weights, tile, blocks, n_groups):
    _, _, depth, cols = tile.shape
    rows = blocks[0].shape[0]
    n_col = len(blocks) // 2
    flat, counts = flattened(blocks)
    width = n_col * rows
    steps = 3
    chunk = depth // steps

    def kernel(place, weights, tile, *refs):
        blocks, refs = refs[: len(flat)], refs[len(flat) :]
        keep, send, left_h, left_l, upper = refs
        step = pl.program_id(0)
        w_re, w_im = weights[0, 0], weights[0, 1]

        def fill(combine):
            held = loaded(blocks, counts, place[4], depth)
            for p in range(n_col):
                at = pl.multiple_of(lax.rem(place[4] + p, n_col) * rows, 16)
                for j, x in enumerate(combine(held[2 * p], held[2 * p + 1])):
                    at_j = slice(j * depth, (j + 1) * depth)
                    left_h[pl.ds(at, rows), at_j], left_l[pl.ds(at, rows), at_j] = halves(x)

        @pl.when(step == 0)
        def _():
            fill(lambda re, im: (-(w_re * im + w_im * re), w_im * im - w_re * re))
            upper[...] = jnp.zeros_like(upper)

        right = halves(jnp.concatenate([tile[0, 0], tile[0, 1]], 0))
        at = [pl.ds(pl.multiple_of(j * depth + step * chunk, 128), chunk) for j in range(2)]
        left = [jnp.concatenate([ref[:, at[0]], ref[:, at[1]]], 1) for ref in (left_h, left_l)]
        total = upper[...] + product(left, right, INNER)
        upper[...] = total

        @pl.when(step == steps - 1)
        def _():
            pairs = total.reshape(n_groups // 2, 2, width // n_groups, cols)
            keep[...] = jnp.where(place[2] == 0, pairs[:, 0], pairs[:, 1])
            send[...] = jnp.where(place[2] == 0, pairs[:, 1], pairs[:, 0])

    part = (n_groups // 2, width // n_groups, cols)

    return pl.pallas_call(
        kernel,
        grid=(steps,),
        in_specs=[SMEM, SMEM, pl.BlockSpec((1, 2, chunk, cols), lambda i: (0, 0, i, 0))]
        + [fixed(x.shape) for x in flat],
        out_specs=[fixed(part)] * 2,
        out_shape=[jax.ShapeDtypeStruct(part, F32)] * 2,
        scratch_shapes=[pltpu.VMEM((width, 2 * depth), BF16)] * 2 + [pltpu.VMEM((width, cols), F32)],
        compiler_params=room(58),
        cost_estimate=QUICK,
    )(place, weights, tile, *flat)


def routing(place, block_owners, n_pole, n_row, n_col, capacity):
    owners_here = n_row * n_col
    devices_all = n_pole * owners_here
    blocks, top = block_owners.shape
    lanes = -(-blocks // 128) * 128
    columns = -(-devices_all // 128) * 128

    def earlier(x, at, axis):
        count = jnp.zeros_like(x)
        for k in range(1, BLOCKS):
            count = count + jnp.where(at >= k, jnp.roll(x, k, axis), 0.0)
        return count

    def kernel(place, owners, slots, source):
        named = jnp.concatenate(
            [owners[...].astype(F32), jnp.full((top, lanes - blocks), -1.0, F32)], 1
        ) if lanes > blocks else owners[...].astype(F32)
        number = lax.broadcasted_iota(jnp.int32, (1, lanes), 1)
        within = lax.rem(number, BLOCKS)
        me = place[5].astype(F32)
        hit = jnp.zeros((1, lanes), F32)
        for t in range(top):
            hit = hit + jnp.where(named[t : t + 1] == me, 1.0, 0.0)
        rank = earlier(hit, within, 1)
        value = (within + 1).astype(F32) * hit
        by_slot = jnp.concatenate(
            [jnp.where(rank == s, value, 0.0) for s in range(capacity)]
            + [jnp.zeros((8 - capacity, lanes), F32)],
            0,
        )
        block = lax.broadcasted_iota(jnp.int32, (lanes, columns), 0)
        group = lax.broadcasted_iota(jnp.int32, (lanes, columns), 1)
        inside = jnp.where((block >= group * BLOCKS) & (block < (group + 1) * BLOCKS), 1.0, 0.0)
        slots[...] = jnp.dot(by_slot, inside, preferred_element_type=F32).astype(jnp.int32)
        block = lax.broadcasted_iota(jnp.int32, (lanes, 128), 0)
        at = lax.broadcasted_iota(jnp.int32, (lanes, 128), 1)
        owner = place[0] * owners_here + lax.broadcasted_iota(jnp.int32, (owners_here, 128), 0)
        local = lax.broadcasted_iota(jnp.int32, (owners_here, 128), 1)
        for d in range(n_pole):
            group = (place[3] * n_pole + (place[0] ^ d)) * n_col + place[4]
            own = jnp.where((block == group * BLOCKS + at) & (at < BLOCKS), 1.0, 0.0)
            here = jnp.dot(named + 1.0, own, preferred_element_type=F32) - 1.0
            hit = jnp.zeros((owners_here, 128), F32)
            for t in range(top):
                hit = hit + jnp.where(here[t : t + 1] == owner.astype(F32), 1.0, 0.0)
            rank = earlier(hit, local, 1)
            value = (local + 1).astype(F32) * hit
            out = jnp.zeros((owners_here, 128), F32)
            for s in range(capacity):
                total = jnp.sum(jnp.where(rank == s, value, 0.0), 1, keepdims=True)
                out = out + jnp.where(local == s, total, 0.0)
            source[d] = out.astype(jnp.int32)

    return pl.pallas_call(
        kernel,
        in_specs=[SMEM, VMEM],
        out_specs=[VMEM] * 2,
        out_shape=[
            jax.ShapeDtypeStruct((8, columns), jnp.int32),
            jax.ShapeDtypeStruct((n_pole, owners_here, 128), jnp.int32),
        ],
        cost_estimate=QUICK,
    )(place, block_owners.T)


def routed_blocks(place, slots, blocks, n_pole, n_row, n_col, capacity):
    _, rows, points = blocks.shape

    def kernel(place, slots, blocks, out):
        for row in range(n_row):
            for col in range(n_col):
                for d in range(n_pole):
                    group = (row * n_pole + (place[0] ^ d)) * n_col + col
                    for s in range(capacity):
                        at = jnp.maximum(slots[s, group] - 1, 0)
                        out[row * n_col + col, d * capacity + s] = blocks[group * BLOCKS + at]

    return pl.pallas_call(
        kernel,
        in_specs=[SMEM, SMEM, VMEM],
        out_specs=VMEM,
        out_shape=jax.ShapeDtypeStruct((n_row * n_col, n_pole * capacity, rows, points), F32),
        cost_estimate=QUICK,
    )(place, slots, blocks)


def charge_terms_plain(place, source, rows, pivots, bases, ancestor):
    n_pole, (n_rows, width) = len(rows), rows[0][0].shape
    n_row, owners, slots, block_rows, points = ancestor.shape
    capacity = slots // n_pole
    left = jnp.concatenate([sum(pivots)] + [sum(x) for x in rows], 0)
    terms = []
    for at_row in range(n_row):
        basis = sum(jnp.where((place[3] ^ b) == at_row, x, 0.0) for b, x in bases.items())
        basis = jnp.roll(basis, place[4], 0)
        basis = basis.reshape(owners, basis.shape[1], -1, points).transpose(0, 2, 1, 3).reshape(owners, width, points)
        result = jnp.einsum("ij,kjg->kig", left, basis, precision=lax.Precision.HIGH)
        total = jnp.sum(result[:, :width] * basis, 1)
        blocks = result[:, width:].reshape(owners, n_pole * BLOCKS, block_rows, points)
        at = source[:, at_row * owners : (at_row + 1) * owners, :capacity].transpose(1, 0, 2) - 1
        place_of = jnp.maximum(at, 0) + jnp.arange(n_pole, dtype=jnp.int32)[None, :, None] * BLOCKS
        found = jax.vmap(lambda x, k: x[k])(blocks, place_of.reshape(owners, slots)) * ancestor[at_row]
        found = jnp.where(at.reshape(owners, slots, 1, 1) >= 0, found, 0.0)
        terms.append(total + jnp.sum(found, (1, 2)))
    return jnp.stack(terms)[:, :, None]


def charge_terms(place, source, rows, pivots, bases, ancestor):
    n_pole, (n_rows, width) = len(rows), rows[0][0].shape
    n_row, owners, slots, block_rows, points = ancestor.shape
    capacity = slots // n_pole
    n_terms = len(rows[0])
    fold = bases[0].shape[2] // points
    if block_rows % 8:
        return charge_terms_plain(place, source, rows, pivots, bases, ancestor)
    order = sorted(bases)
    n_groups = len(order)

    def kernel(place, source, *refs):
        rows, pivots, refs = refs[: n_pole * n_terms], refs[n_pole * n_terms :][:n_pole], refs[n_pole * (n_terms + 1) :]
        rows = [sum(ref[...] for ref in rows[d * n_terms : (d + 1) * n_terms]) for d in range(n_pole)]
        ancestor, bases, (out, held) = refs[0], refs[1 : 1 + n_groups], refs[1 + n_groups :]
        pivot = pivots[0][...]
        for ref in pivots[1:]:
            pivot = pivot + ref[...]
        left = halves(jnp.concatenate([pivot] + rows, 0))
        for g, b in enumerate(order):
            at_row = place[3] ^ b
            basis = jnp.concatenate(
                [
                    jnp.concatenate([bases[g][k, :, f * points : (f + 1) * points] for f in range(fold)], 0)
                    for k in range(owners)
                ],
                1,
            )
            result = product(left, halves(basis), INNER)
            held[...] = result[width:]
            sums = jnp.sum(result[:width] * basis, 0, keepdims=True)
            for k in range(owners):
                o = lax.rem(place[4] + k, owners)
                lanes = slice(k * points, (k + 1) * points)
                found = jnp.zeros((block_rows, points), F32)
                for d in range(n_pole):
                    for s in range(capacity):
                        at = source[d, at_row * owners + o, s] - 1
                        first = pl.multiple_of(d * n_rows + jnp.maximum(at, 0) * block_rows, block_rows)
                        block = held[pl.ds(first, block_rows), lanes] * ancestor[at_row, o, d * capacity + s]
                        found = found + jnp.where(at >= 0, block, 0.0)
                out[at_row, o] = sums[:, lanes] + jnp.sum(found, 0, keepdims=True)

    return pl.pallas_call(
        kernel,
        in_specs=[SMEM, SMEM] + [VMEM] * (n_pole * (n_terms + 1) + 1 + n_groups),
        out_specs=VMEM,
        out_shape=jax.ShapeDtypeStruct((n_row, owners, 1, points), F32),
        scratch_shapes=[pltpu.VMEM((n_pole * n_rows, owners * points), F32)],
        compiler_params=room(24),
        cost_estimate=QUICK,
    )(place, source, *[x for terms in rows for x in terms], *pivots, ancestor, *[bases[k] for k in order])


def permute(x, axis, pairs):
    return lax.ppermute(x, axis, pairs)


def swap(x, axis, mask):
    return lax.ppermute(x, axis, [(i, i ^ mask) for i in range(lax.axis_size(axis))])


def shift(x, axis, by):
    n = lax.axis_size(axis)
    return lax.ppermute(x, axis, [(i, (i + by) % n) for i in range(n)])


def gather_swapped(x, axis, first):
    n = lax.axis_size(axis)
    held = {0: x}
    bit = n // 2
    while bit:
        for d in list(held):
            held[d ^ bit] = swap(after(held[d], *first) if d else x, axis, bit)
        bit //= 2
    return [held[d] for d in range(n)]


def gather_near(x, axis):
    n = lax.axis_size(axis)
    return [shift(x, axis, -p) for p in (range(1, n) if n != 4 else (1, 3))]


def gather_cyclic(x, near, axis):
    if lax.axis_size(axis) != 4:
        return [x] + near
    one, three = near
    leftward = permute(one, axis, [(2, 1), (1, 0)])
    rightward = permute(three, axis, [(1, 2), (2, 3)])
    return [x, one, (leftward, rightward), three]


def joined(blocks, axis):
    return [jnp.where(lax.axis_index(axis) < 2, x[0], x[1]) if isinstance(x, tuple) else x for x in blocks]


def reduce_scatter_swapped(x, axis, masks):
    total = x[0]
    for term, mask in zip(x[1:], masks, strict=True):
        total = total + swap(term, axis, mask)
    return total


def pick(x, at):
    return lax.dynamic_index_in_dim(x, at, 0, keepdims=False)


def gather_all(x, axes):
    n = 1
    for axis in axes:
        n *= lax.axis_size(axis)
    spread = jnp.broadcast_to(x[None], (n,) + x.shape)
    return lax.all_to_all(spread, axes, split_axis=0, concat_axis=0, tiled=True)


def after(x, *others):
    return lax.optimization_barrier((x,) + others)[0]


def swap_both(x, axes, masks):
    first, second = (lax.axis_size(a) for a in axes)
    pairs = [
        (i * second + j, (i ^ masks[0]) * second + (j ^ masks[1])) for i in range(first) for j in range(second)
    ]
    return lax.ppermute(x, axes, pairs)


def rows_by_pole(x, before, later):
    n_pole, n_col = lax.axis_size("pole"), lax.axis_size("col")
    me = lax.axis_index("col")
    held = [pick(x, me ^ d) for d in range(n_col)]
    bit = 1
    while bit < n_col:
        away = [d for d in range(0, n_col, bit) if d & bit]
        if bit == 2 and n_col == 4:
            mine, other = held[0], held[2]
            later = after(later, other)
            rows = [[mine, swap(other, "col", 2)]]
            for d in range(1, n_pole):
                rows.append([swap(mine, "pole", d), swap_both(other, ("pole", "col"), (d, 2))])
            return rows, later
        arrived = swap(jnp.stack([held[d] for d in away]), "col", bit)
        if bit == 1:
            arrived = after(arrived, *before)
        for j, d in enumerate(away):
            held[d ^ bit] = held[d ^ bit] + arrived[j]
        bit *= 2
    return [[held[0]]] + [[swap(held[0], "pole", d)] for d in range(1, n_pole)], later


def body(
    inverse_tile,
    lower_factor,
    upper_factor,
    pivot_inverse,
    pole_weights,
    block_owners,
    basis_ancestor,
    basis_super,
):
    n_pole, n_row, n_col = (lax.axis_size(a) for a in ("pole", "row", "col"))
    pole, row, col = (lax.axis_index(a) for a in ("pole", "row", "col"))
    devices_all = n_pole * n_row * n_col
    tile_rows, tile_cols = inverse_tile.shape[2:]
    width, points = basis_super.shape
    capacity = max(2, (BLOCKS * block_owners.shape[1] + devices_all - 1) // devices_all)
    piece = upper_factor.shape[2]
    rows_here = tile_rows // (n_pole * n_col)
    block_rows = rows_here // BLOCKS
    out_rows = width // (n_pole * n_row)
    groups = n_row * n_pole * n_col
    me = (pole * n_row + row) * n_col + col
    position = (row * n_pole + pole) * n_col + col
    place = jnp.stack([pole, row // 2, row % 2, row, col, me, position]).astype(jnp.int32)

    fold = width // piece
    basis = basis_super.reshape(fold, piece, points).transpose(1, 0, 2).reshape(piece, fold * points)
    upper_own = [upper_factor[0, 0], jnp.concatenate([upper_factor[0, 1], basis], 1)]
    upper_near = [gather_near(x, "col") for x in upper_own]

    slots, source = routing(place, block_owners, n_pole, n_row, n_col, capacity)
    ancestor = routed_blocks(
        place, slots, basis_ancestor.reshape(groups * BLOCKS, block_rows, points), n_pole, n_row, n_col, capacity
    )
    lower = gather_swapped(lower_factor[0], "row", (ancestor, *upper_near[0]))


    parts, beside = lower_products(place, pole_weights, inverse_tile, lower, n_pole)
    upper = [
        gather_cyclic(upper_own[0], upper_near[0], "col"),
        gather_cyclic(upper_own[1], [after(x, parts[0]) for x in upper_near[1]], "col"),
    ]
    ancestor = lax.all_to_all(
        after(ancestor, parts[0], upper_near[1][-1]), ("row", "col"), split_axis=0, concat_axis=0, tiled=True
    ).reshape(n_row, n_col, -1, block_rows, points)
    half = reduce_scatter_swapped(parts, "pole", list(range(1, n_pole)))

    line = jnp.stack(joined([jax.tree.map(lambda y: y[:, tile_rows:], x) for x in upper[1]], "col"))
    bases = {b: swap(line, "row", b) if b else line for b in range(0, n_row, 2)}
    upper = [x for pair in zip(*upper, strict=True) for x in pair]

    pivot = pivot_term(place, pole_weights, upper, beside, after(pivot_inverse, half))
    pivots = [pivot] + [swap(pivot, "pole", d) for d in range(1, n_pole)]
    keep, send = upper_products(place, after(pole_weights, pivot), inverse_tile, upper, n_pole * n_row)
    for b in list(bases):
        bases[b + 1] = swap(bases[b], "row", 1)
    rows, send = rows_by_pole(half.reshape(n_col, rows_here, width), (keep,), send)
    near = (keep + swap(send, "row", 1)).reshape(n_pole, n_row // 2, -1, tile_cols)
    upper_density, arrived = 0.0, []
    for a in range(n_pole):
        for b in range(n_row // 2):
            part = pick(pick(near, pole ^ a), (row // 2) ^ b)
            if a or b:
                arrived.append(swap_both(part, ("pole", "row"), (a, 2 * b)))
            else:
                upper_density = part

    terms = charge_terms(place, source, rows, pivots, bases, ancestor)
    terms = lax.all_to_all(
        after(terms, *arrived).reshape(n_row * n_col, 1, points),
        ("row", "col"),
        split_axis=0,
        concat_axis=0,
        tiled=True,
    )
    return (upper_density + sum(arrived), jnp.sum(terms, (0, 1)))


def solution(mesh):
    placed = (
        P("pole", None, "row", "col"),
        P("pole", None, "row", "col"),
        P("pole", None, "col", "row"),
        P("pole", None, "row", "col"),
        P("pole", None),
        P(),
        P(None, ("pole", "row", "col")),
        P(None, ("pole", "row", "col")),
    )
    return jax.shard_map(
        body,
        mesh=mesh,
        in_specs=placed,
        out_specs=(P(("pole", "row"), "col"), P(("pole", "row", "col"))),
        check_vma=False,
    )
```

```python
import jax
import jax.numpy as jnp
from jax import lax
from jax.experimental import pallas as pl
from jax.experimental.pallas import tpu as pltpu
from jax.sharding import PartitionSpec as P

BLOCKS = 18
HIGH = lax.Precision.HIGH
F32, BF16 = jnp.float32, jnp.bfloat16
LAST, INNER = ((1,), (1,)), ((1,), (0,))
SMEM = pl.BlockSpec(memory_space=pltpu.SMEM)
VMEM = pl.BlockSpec(memory_space=pltpu.VMEM)


def room(mebibytes):
    return pltpu.CompilerParams(vmem_limit_bytes=mebibytes * 2**20)


def halves(x):
    high = x.astype(BF16)
    return high, (x - high.astype(F32)).astype(BF16)


def product(left, right, contract):
    def one(a, b):
        return lax.dot_general(a, b, (contract, ((), ())), preferred_element_type=F32)

    return one(left[0], right[0]) + (one(left[0], right[1]) + one(left[1], right[0]))


QUICK = pl.CostEstimate(flops=0, bytes_accessed=0, transcendentals=0)


def fixed(shape):
    return pl.BlockSpec(shape, lambda i: (0,) * len(shape))


def lower_products(place, weights, tile, blocks, n_pole):
    _, _, rows, depth = tile.shape
    piece = blocks[0].shape[1]
    n_row = len(blocks)
    width = n_row * piece
    steps = 3
    chunk = rows // steps
    part = rows // n_pole

    def kernel(place, weights, tile, *refs):
        blocks, refs = refs[:n_row], refs[n_row:]
        outs, (out_h, out_l, right_h, right_l, whole) = refs[:n_pole], refs[n_pole:]
        step = pl.program_id(0)

        @pl.when(step == 0)
        def _():
            w_re, w_im = weights[0, 0], weights[0, 1]
            for d in range(n_row):
                re, im = blocks[d][0], blocks[d][1]
                re, im = w_re * re - w_im * im, w_re * im + w_im * re
                for side, pair in enumerate(((-im, -re), (re, -im))):
                    at = pl.multiple_of(side * width + (place[3] ^ d) * piece, 16)
                    for j, x in enumerate(pair):
                        cols = slice(j * depth, (j + 1) * depth)
                        right_h[pl.ds(at, piece), cols], right_l[pl.ds(at, piece), cols] = halves(x)

        left = halves(jnp.concatenate([tile[0, 0], tile[0, 1]], 1))
        out = product(left, (right_h[...], right_l[...]), LAST)
        out_h[...], out_l[...] = halves(out)
        whole[pl.ds(pl.multiple_of(step * chunk, 16), chunk), :] = out[:, :width]

        @pl.when(step == steps - 1)
        def _():
            for d in range(n_pole):
                at = pl.multiple_of((place[0] ^ d) * part, 8)
                outs[d][...] = whole[pl.ds(at, part), :]

    out = pl.pallas_call(
        kernel,
        grid=(steps,),
        in_specs=[SMEM, SMEM, pl.BlockSpec((1, 2, chunk, depth), lambda i: (0, 0, i, 0))]
        + [fixed(blocks[0].shape)] * n_row,
        out_specs=[fixed((part, width))] * n_pole + [pl.BlockSpec((chunk, 2 * width), lambda i: (i, 0))] * 2,
        out_shape=[jax.ShapeDtypeStruct((part, width), F32)] * n_pole
        + [jax.ShapeDtypeStruct((rows, 2 * width), BF16)] * 2,
        scratch_shapes=[pltpu.VMEM((2 * width, 2 * depth), BF16)] * 2 + [pltpu.VMEM((rows, width), F32)],
        compiler_params=room(58),
        cost_estimate=QUICK,
    )(place, weights, tile, *blocks)
    return out[:n_pole], out[n_pole:]


def flattened(blocks):
    pairs = [x if isinstance(x, tuple) else (x,) for x in blocks]
    return [y for x in pairs for y in x], [len(x) for x in pairs]


def loaded(refs, counts, col, depth):
    out, at = [], 0
    for count in counts:
        x = refs[at][:, :depth]
        out.append(x if count == 1 else jnp.where(col < 2, x, refs[at + 1][:, :depth]))
        at += count
    return out


def pivot_term(place, weights, blocks, lower, pivot_inverse):
    rows = blocks[0].shape[0]
    n_col = len(blocks) // 2
    flat, counts = flattened(blocks)
    width = n_col * rows
    depth = lower[0].shape[0]
    piece_rows, piece_cols = pivot_inverse.shape[2:]

    def kernel(place, weights, *refs):
        blocks, refs = refs[: len(flat)], refs[len(flat) :]
        lower_h, lower_l, inverse, pivot, left_h, left_l = refs
        blocks = loaded(blocks, counts, place[4], depth)
        for p in range(n_col):
            at = pl.multiple_of(lax.rem(place[4] + p, n_col) * rows, 16)
            for j, x in enumerate((-blocks[2 * p], blocks[2 * p + 1])):
                at_j = slice(j * depth, (j + 1) * depth)
                left_h[pl.ds(at, rows), at_j], left_l[pl.ds(at, rows), at_j] = halves(x)
        right = [jnp.concatenate([x[:, :width], x[:, width:]], 0) for x in (lower_h, lower_l)]
        pivot[...] = product((left_h[...], left_l[...]), right, INNER)
        at = pl.multiple_of(place[3] * piece_rows, 8)
        own = weights[0, 0] * inverse[0, 1] + weights[0, 1] * inverse[0, 0]
        for k in range(n_col):

            @pl.when(place[4] == k)
            def _():
                pivot[pl.ds(at, piece_rows), k * piece_cols : (k + 1) * piece_cols] += own

    return pl.pallas_call(
        kernel,
        grid=(1,),
        in_specs=[SMEM, SMEM]
        + [fixed(x.shape) for x in flat]
        + [fixed(lower[0].shape)] * 2
        + [fixed(pivot_inverse.shape)],
        out_specs=fixed((width, width)),
        out_shape=jax.ShapeDtypeStruct((width, width), F32),
        scratch_shapes=[pltpu.VMEM((width, 2 * depth), BF16)] * 2,
        compiler_params=room(58),
        cost_estimate=QUICK,
    )(place, weights, *flat, *lower, pivot_inverse)


def upper_products(place, weights, tile, blocks, n_groups):
    _, _, depth, cols = tile.shape
    rows = blocks[0].shape[0]
    n_col = len(blocks) // 2
    flat, counts = flattened(blocks)
    width = n_col * rows
    steps = 3
    chunk = depth // steps

    def kernel(place, weights, tile, *refs):
        blocks, refs = refs[: len(flat)], refs[len(flat) :]
        keep, send, left_h, left_l, upper = refs
        step = pl.program_id(0)
        w_re, w_im = weights[0, 0], weights[0, 1]

        def fill(combine):
            held = loaded(blocks, counts, place[4], depth)
            for p in range(n_col):
                at = pl.multiple_of(lax.rem(place[4] + p, n_col) * rows, 16)
                for j, x in enumerate(combine(held[2 * p], held[2 * p + 1])):
                    at_j = slice(j * depth, (j + 1) * depth)
                    left_h[pl.ds(at, rows), at_j], left_l[pl.ds(at, rows), at_j] = halves(x)

        @pl.when(step == 0)
        def _():
            fill(lambda re, im: (-(w_re * im + w_im * re), w_im * im - w_re * re))
            upper[...] = jnp.zeros_like(upper)

        right = halves(jnp.concatenate([tile[0, 0], tile[0, 1]], 0))
        at = [pl.ds(pl.multiple_of(j * depth + step * chunk, 128), chunk) for j in range(2)]
        left = [jnp.concatenate([ref[:, at[0]], ref[:, at[1]]], 1) for ref in (left_h, left_l)]
        total = upper[...] + product(left, right, INNER)
        upper[...] = total

        @pl.when(step == steps - 1)
        def _():
            pairs = total.reshape(n_groups // 2, 2, width // n_groups, cols)
            keep[...] = jnp.where(place[2] == 0, pairs[:, 0], pairs[:, 1])
            send[...] = jnp.where(place[2] == 0, pairs[:, 1], pairs[:, 0])

    part = (n_groups // 2, width // n_groups, cols)

    return pl.pallas_call(
        kernel,
        grid=(steps,),
        in_specs=[SMEM, SMEM, pl.BlockSpec((1, 2, chunk, cols), lambda i: (0, 0, i, 0))]
        + [fixed(x.shape) for x in flat],
        out_specs=[fixed(part)] * 2,
        out_shape=[jax.ShapeDtypeStruct(part, F32)] * 2,
        scratch_shapes=[pltpu.VMEM((width, 2 * depth), BF16)] * 2 + [pltpu.VMEM((width, cols), F32)],
        compiler_params=room(58),
        cost_estimate=QUICK,
    )(place, weights, tile, *flat)


def routing(place, block_owners, n_pole, n_row, n_col, capacity):
    owners_here = n_row * n_col
    devices_all = n_pole * owners_here
    blocks, top = block_owners.shape
    lanes = -(-blocks // 128) * 128
    columns = -(-devices_all // 128) * 128

    def earlier(x, at, axis):
        count = jnp.zeros_like(x)
        for k in range(1, BLOCKS):
            count = count + jnp.where(at >= k, jnp.roll(x, k, axis), 0.0)
        return count

    def kernel(place, owners, slots, source):
        named = jnp.concatenate(
            [owners[...].astype(F32), jnp.full((top, lanes - blocks), -1.0, F32)], 1
        ) if lanes > blocks else owners[...].astype(F32)
        number = lax.broadcasted_iota(jnp.int32, (1, lanes), 1)
        within = lax.rem(number, BLOCKS)
        me = place[5].astype(F32)
        hit = jnp.zeros((1, lanes), F32)
        for t in range(top):
            hit = hit + jnp.where(named[t : t + 1] == me, 1.0, 0.0)
        rank = earlier(hit, within, 1)
        value = (within + 1).astype(F32) * hit
        by_slot = jnp.concatenate(
            [jnp.where(rank == s, value, 0.0) for s in range(capacity)]
            + [jnp.zeros((8 - capacity, lanes), F32)],
            0,
        )
        block = lax.broadcasted_iota(jnp.int32, (lanes, columns), 0)
        group = lax.broadcasted_iota(jnp.int32, (lanes, columns), 1)
        inside = jnp.where((block >= group * BLOCKS) & (block < (group + 1) * BLOCKS), 1.0, 0.0)
        slots[...] = jnp.dot(by_slot, inside, preferred_element_type=F32).astype(jnp.int32)
        block = lax.broadcasted_iota(jnp.int32, (lanes, 128), 0)
        at = lax.broadcasted_iota(jnp.int32, (lanes, 128), 1)
        owner = place[0] * owners_here + lax.broadcasted_iota(jnp.int32, (owners_here, 128), 0)
        local = lax.broadcasted_iota(jnp.int32, (owners_here, 128), 1)
        for d in range(n_pole):
            group = (place[3] * n_pole + (place[0] ^ d)) * n_col + place[4]
            own = jnp.where((block == group * BLOCKS + at) & (at < BLOCKS), 1.0, 0.0)
            here = jnp.dot(named + 1.0, own, preferred_element_type=F32) - 1.0
            hit = jnp.zeros((owners_here, 128), F32)
            for t in range(top):
                hit = hit + jnp.where(here[t : t + 1] == owner.astype(F32), 1.0, 0.0)
            rank = earlier(hit, local, 1)
            value = (local + 1).astype(F32) * hit
            out = jnp.zeros((owners_here, 128), F32)
            for s in range(capacity):
                total = jnp.sum(jnp.where(rank == s, value, 0.0), 1, keepdims=True)
                out = out + jnp.where(local == s, total, 0.0)
            source[d] = out.astype(jnp.int32)

    return pl.pallas_call(
        kernel,
        in_specs=[SMEM, VMEM],
        out_specs=[VMEM] * 2,
        out_shape=[
            jax.ShapeDtypeStruct((8, columns), jnp.int32),
            jax.ShapeDtypeStruct((n_pole, owners_here, 128), jnp.int32),
        ],
        cost_estimate=QUICK,
    )(place, block_owners.T)


def routed_blocks(place, slots, blocks, n_pole, n_row, n_col, capacity):
    _, rows, points = blocks.shape

    def kernel(place, slots, blocks, out):
        for row in range(n_row):
            for col in range(n_col):
                for d in range(n_pole):
                    group = (row * n_pole + (place[0] ^ d)) * n_col + col
                    for s in range(capacity):
                        at = jnp.maximum(slots[s, group] - 1, 0)
                        out[row * n_col + col, d * capacity + s] = blocks[group * BLOCKS + at]

    return pl.pallas_call(
        kernel,
        in_specs=[SMEM, SMEM, VMEM],
        out_specs=VMEM,
        out_shape=jax.ShapeDtypeStruct((n_row * n_col, n_pole * capacity, rows, points), F32),
        cost_estimate=QUICK,
    )(place, slots, blocks)


def charge_terms_plain(place, source, rows, pivots, bases, ancestor):
    n_pole, (n_rows, width) = len(rows), rows[0][0].shape
    n_row, owners, slots, block_rows, points = ancestor.shape
    capacity = slots // n_pole
    left = jnp.concatenate([sum(pivots)] + [sum(x) for x in rows], 0)
    terms = []
    for at_row in range(n_row):
        basis = sum(jnp.where((place[3] ^ b) == at_row, x, 0.0) for b, x in bases.items())
        basis = jnp.roll(basis, place[4], 0)
        basis = basis.reshape(owners, basis.shape[1], -1, points).transpose(0, 2, 1, 3).reshape(owners, width, points)
        result = jnp.einsum("ij,kjg->kig", left, basis, precision=lax.Precision.HIGH)
        total = jnp.sum(result[:, :width] * basis, 1)
        blocks = result[:, width:].reshape(owners, n_pole * BLOCKS, block_rows, points)
        at = source[:, at_row * owners : (at_row + 1) * owners, :capacity].transpose(1, 0, 2) - 1
        place_of = jnp.maximum(at, 0) + jnp.arange(n_pole, dtype=jnp.int32)[None, :, None] * BLOCKS
        found = jax.vmap(lambda x, k: x[k])(blocks, place_of.reshape(owners, slots)) * ancestor[at_row]
        found = jnp.where(at.reshape(owners, slots, 1, 1) >= 0, found, 0.0)
        terms.append(total + jnp.sum(found, (1, 2)))
    return jnp.stack(terms)[:, :, None]


def charge_terms(place, source, rows, pivots, bases, ancestor):
    n_pole, (n_rows, width) = len(rows), rows[0][0].shape
    n_row, owners, slots, block_rows, points = ancestor.shape
    capacity = slots // n_pole
    n_terms = len(rows[0])
    fold = bases[0].shape[2] // points
    if block_rows % 8:
        return charge_terms_plain(place, source, rows, pivots, bases, ancestor)
    order = sorted(bases)
    n_groups = len(order)

    def kernel(place, source, *refs):
        rows, pivots, refs = refs[: n_pole * n_terms], refs[n_pole * n_terms :][:n_pole], refs[n_pole * (n_terms + 1) :]
        rows = [sum(ref[...] for ref in rows[d * n_terms : (d + 1) * n_terms]) for d in range(n_pole)]
        ancestor, bases, (out, held) = refs[0], refs[1 : 1 + n_groups], refs[1 + n_groups :]
        pivot = pivots[0][...]
        for ref in pivots[1:]:
            pivot = pivot + ref[...]
        left = halves(jnp.concatenate([pivot] + rows, 0))
        for g, b in enumerate(order):
            at_row = place[3] ^ b
            basis = jnp.concatenate(
                [
                    jnp.concatenate([bases[g][k, :, f * points : (f + 1) * points] for f in range(fold)], 0)
                    for k in range(owners)
                ],
                1,
            )
            result = product(left, halves(basis), INNER)
            held[...] = result[width:]
            sums = jnp.sum(result[:width] * basis, 0, keepdims=True)
            for k in range(owners):
                o = lax.rem(place[4] + k, owners)
                lanes = slice(k * points, (k + 1) * points)
                found = jnp.zeros((block_rows, points), F32)
                for d in range(n_pole):
                    for s in range(capacity):
                        at = source[d, at_row * owners + o, s] - 1
                        first = pl.multiple_of(d * n_rows + jnp.maximum(at, 0) * block_rows, block_rows)
                        block = held[pl.ds(first, block_rows), lanes] * ancestor[at_row, o, d * capacity + s]
                        found = found + jnp.where(at >= 0, block, 0.0)
                out[at_row, o] = sums[:, lanes] + jnp.sum(found, 0, keepdims=True)

    return pl.pallas_call(
        kernel,
        in_specs=[SMEM, SMEM] + [VMEM] * (n_pole * (n_terms + 1) + 1 + n_groups),
        out_specs=VMEM,
        out_shape=jax.ShapeDtypeStruct((n_row, owners, 1, points), F32),
        scratch_shapes=[pltpu.VMEM((n_pole * n_rows, owners * points), F32)],
        compiler_params=room(58),
        cost_estimate=QUICK,
    )(place, source, *[x for terms in rows for x in terms], *pivots, ancestor, *[bases[k] for k in order])


def permute(x, axis, pairs):
    return lax.ppermute(x, axis, pairs)


def swap(x, axis, mask):
    return lax.ppermute(x, axis, [(i, i ^ mask) for i in range(lax.axis_size(axis))])


def shift(x, axis, by):
    n = lax.axis_size(axis)
    return lax.ppermute(x, axis, [(i, (i + by) % n) for i in range(n)])


def gather_swapped(x, axis, first):
    n = lax.axis_size(axis)
    held = {0: x}
    bit = n // 2
    while bit:
        for d in list(held):
            held[d ^ bit] = swap(after(held[d], *first) if d else x, axis, bit)
        bit //= 2
    return [held[d] for d in range(n)]


def gather_near(x, axis):
    n = lax.axis_size(axis)
    return [shift(x, axis, -p) for p in (range(1, n) if n != 4 else (1, 3))]


def gather_cyclic(x, near, axis):
    if lax.axis_size(axis) != 4:
        return [x] + near
    one, three = near
    leftward = permute(one, axis, [(2, 1), (1, 0)])
    rightward = permute(three, axis, [(1, 2), (2, 3)])
    return [x, one, (leftward, rightward), three]


def joined(blocks, axis):
    return [jnp.where(lax.axis_index(axis) < 2, x[0], x[1]) if isinstance(x, tuple) else x for x in blocks]


def reduce_scatter_swapped(x, axis, masks):
    total = x[0]
    for term, mask in zip(x[1:], masks, strict=True):
        total = total + swap(term, axis, mask)
    return total


def pick(x, at):
    return lax.dynamic_index_in_dim(x, at, 0, keepdims=False)


def gather_all(x, axes):
    n = 1
    for axis in axes:
        n *= lax.axis_size(axis)
    spread = jnp.broadcast_to(x[None], (n,) + x.shape)
    return lax.all_to_all(spread, axes, split_axis=0, concat_axis=0, tiled=True)


def after(x, *others):
    return lax.optimization_barrier((x,) + others)[0]


def swap_both(x, axes, masks):
    first, second = (lax.axis_size(a) for a in axes)
    pairs = [
        (i * second + j, (i ^ masks[0]) * second + (j ^ masks[1])) for i in range(first) for j in range(second)
    ]
    return lax.ppermute(x, axes, pairs)


def rows_by_pole(x, before, between):
    n_pole, n_col = lax.axis_size("pole"), lax.axis_size("col")
    me = lax.axis_index("col")
    held = [pick(x, me ^ d) for d in range(n_col)]
    bit = 1
    while bit < n_col:
        away = [d for d in range(0, n_col, bit) if d & bit]
        if bit == 2 and n_col == 4:
            mine, other = held[0], held[2]
            other = after(other, between)
            rows = [[mine, swap(other, "col", 2)]]
            for d in range(1, n_pole):
                rows.append([swap(mine, "pole", d), swap_both(other, ("pole", "col"), (d, 2))])
            return rows
        arrived = swap(jnp.stack([held[d] for d in away]), "col", bit)
        if bit == 1:
            arrived = after(arrived, before)
        for j, d in enumerate(away):
            held[d ^ bit] = held[d ^ bit] + arrived[j]
        bit *= 2
    return [[held[0]]] + [[swap(held[0], "pole", d)] for d in range(1, n_pole)]


def body(
    inverse_tile,
    lower_factor,
    upper_factor,
    pivot_inverse,
    pole_weights,
    block_owners,
    basis_ancestor,
    basis_super,
):
    n_pole, n_row, n_col = (lax.axis_size(a) for a in ("pole", "row", "col"))
    pole, row, col = (lax.axis_index(a) for a in ("pole", "row", "col"))
    devices_all = n_pole * n_row * n_col
    tile_rows, tile_cols = inverse_tile.shape[2:]
    width, points = basis_super.shape
    capacity = max(2, (BLOCKS * block_owners.shape[1] + devices_all - 1) // devices_all)
    piece = upper_factor.shape[2]
    rows_here = tile_rows // (n_pole * n_col)
    block_rows = rows_here // BLOCKS
    out_rows = width // (n_pole * n_row)
    groups = n_row * n_pole * n_col
    me = (pole * n_row + row) * n_col + col
    position = (row * n_pole + pole) * n_col + col
    place = jnp.stack([pole, row // 2, row % 2, row, col, me, position]).astype(jnp.int32)

    fold = width // piece
    basis = basis_super.reshape(fold, piece, points).transpose(1, 0, 2).reshape(piece, fold * points)
    upper_own = [upper_factor[0, 0], jnp.concatenate([upper_factor[0, 1], basis], 1)]
    upper_near = [gather_near(x, "col") for x in upper_own]

    slots, source = routing(place, block_owners, n_pole, n_row, n_col, capacity)
    ancestor = routed_blocks(
        place, slots, basis_ancestor.reshape(groups * BLOCKS, block_rows, points), n_pole, n_row, n_col, capacity
    )
    lower = gather_swapped(lower_factor[0], "row", (ancestor, *upper_near[0]))


    parts, beside = lower_products(place, pole_weights, inverse_tile, lower, n_pole)
    upper = [
        gather_cyclic(upper_own[0], upper_near[0], "col"),
        gather_cyclic(upper_own[1], [after(x, parts[0]) for x in upper_near[1]], "col"),
    ]
    ancestor = lax.all_to_all(
        after(ancestor, parts[0], upper_near[1][-1]), ("row", "col"), split_axis=0, concat_axis=0, tiled=True
    ).reshape(n_row, n_col, -1, block_rows, points)
    half = reduce_scatter_swapped(parts, "pole", list(range(1, n_pole)))

    line = jnp.stack(joined([jax.tree.map(lambda y: y[:, tile_rows:], x) for x in upper[1]], "col"))
    bases = {b: swap(line, "row", b) if b else line for b in range(0, n_row, 2)}
    upper = [x for pair in zip(*upper, strict=True) for x in pair]

    pivot = pivot_term(place, pole_weights, upper, beside, after(pivot_inverse, half))
    pivots = [pivot] + [swap(pivot, "pole", d) for d in range(1, n_pole)]
    keep, send = upper_products(place, after(pole_weights, pivot), inverse_tile, upper, n_pole * n_row)
    for b in list(bases):
        bases[b + 1] = swap(bases[b], "row", 1)
    near = (keep + swap(send, "row", 1)).reshape(n_pole, n_row // 2, -1, tile_cols)
    rows = rows_by_pole(half.reshape(n_col, rows_here, width), keep, near)
    upper_density, arrived = 0.0, []
    for a in range(n_pole):
        for b in range(n_row // 2):
            part = pick(pick(near, pole ^ a), (row // 2) ^ b)
            if a or b:
                arrived.append(swap_both(part, ("pole", "row"), (a, 2 * b)))
            else:
                upper_density = part

    terms = charge_terms(place, source, rows, pivots, bases, ancestor)
    terms = lax.all_to_all(
        after(terms, *arrived).reshape(n_row * n_col, 1, points),
        ("row", "col"),
        split_axis=0,
        concat_axis=0,
        tiled=True,
    )
    return (upper_density + sum(arrived), jnp.sum(terms, (0, 1)))


def solution(mesh):
    placed = (
        P("pole", None, "row", "col"),
        P("pole", None, "row", "col"),
        P("pole", None, "col", "row"),
        P("pole", None, "row", "col"),
        P("pole", None),
        P(),
        P(None, ("pole", "row", "col")),
        P(None, ("pole", "row", "col")),
    )
    return jax.shard_map(
        body,
        mesh=mesh,
        in_specs=placed,
        out_specs=(P(("pole", "row"), "col"), P(("pole", "row", "col"))),
        check_vma=False,
    )
```
